128 devices in a mesh: slab: 16 (over x_lo, y, core), angle: 8 (over z, x_hi).
Axes of the slice: x: 4 (x_hi: 2, x_lo: 2; x = x_hi * 2 + x_lo), y: 4, z: 4, core: 2. Of those that a mesh axis runs over, the one named last changes fastest.
Arguments:
- fields: float32 [8, 2, 2, 3, 64, 128, 128], P('angle', None, None, None, 'slab'), may hold values from -6 to 6
- spectra: float32 [8, 2, 2, 3, 64, 128, 128], P('angle', None, None, None, 'slab'), may hold values from -6 to 6
- inv_eps: float32 [64, 128, 128], P('slab'), may hold values from 0.15 to 1
- step_phase: float32 [2], replicated, may hold values from -3.140625 to 3.140625
Outputs:
- fields_out: float32 [8, 2, 2, 3, 64, 128, 128], P('angle', None, None, None, 'slab')
- spectra_out: float32 [8, 2, 2, 3, 64, 128, 128], P('angle', None, None, None, 'slab')
- gradient: float32 [8, 128, 128], P(None, 'slab')
The draws below stay inside these ranges and needn't reach their ends.
All inputs are finite; a program needn't handle non-finite values.
Results may differ from the reference program's by a relative error of at most 0.00007.
Values sent between devices are 32-bit elements; how exact they have to be, the bound alone decides.
A program may use at most 64 MiB of HBM per device.

```python
import math
import jax
import jax.numpy as jnp
from jax import lax

NX = 128
NY = 128
DZ = 8
STEPS = 2
NZ = 64
ANGLES = 8


def levels(rng, shape, split, low, high):
    def one(dim, parts):
        draws = jax.random.uniform(jax.random.fold_in(jax.random.fold_in(rng, 6), dim), (parts,), jnp.float32, low / len(split), high / len(split))
        return jnp.repeat(jnp.exp(draws), shape[dim] // parts).reshape((-1,) + (1,) * (len(shape) - dim - 1))

    level = one(*split[0])
    for cut in split[1:]:
        level = level * one(*cut)
    return level


def centred(stream_key, dims, spread, limit, shards=(), dtype=jnp.bfloat16):
    factor_of = levels(stream_key, dims, shards, -0.22, 0.18) if shards else 1.0
    values = jax.random.normal(stream_key, dims, jnp.float32) * spread * factor_of
    return jnp.minimum(jnp.maximum(values, -limit), limit).astype(dtype)


def setup_inputs(seed: int = 0) -> dict:
    splits = jax.random.split(jax.random.key(seed), 5)
    return {
        "fields": centred(splits[0], (ANGLES, 2, 2, 3, NZ, NX, NY), 1.0, 6.0, ((0, 8), (4, 16)), jnp.float32),
        "spectra": centred(splits[1], (ANGLES, 2, 2, 3, NZ, NX, NY), 1.0, 6.0, ((0, 8), (4, 16)), jnp.float32),
        "inv_eps": jnp.clip(jnp.exp(math.log(1.0) - 1.89712 * jax.random.uniform(splits[2], (NZ, NX, NY), jnp.float32) ** levels(splits[2], (NZ, NX, NY), ((0, 16),), -0.2, 0.2)), 0.15, 1.0),
        "step_phase": jnp.clip(jax.random.uniform(splits[3], (STEPS,), jnp.float32, -3.140625, 3.140625), -3.140625, 3.140625),
    }


COURANT = 0.5
FILTER_TAPS = (0.0625, 0.25, 0.375, 0.25, 0.0625)


def ahead_diff(array_in, along_axis):
    length = array_in.shape[along_axis]
    shifted = jnp.concatenate([lax.slice_in_dim(array_in, 1, length, axis=along_axis), jnp.zeros_like(lax.slice_in_dim(array_in, 0, 1, axis=along_axis))], axis=along_axis)
    return shifted - array_in


def behind_diff(array_in, along_axis):
    length = array_in.shape[along_axis]
    shifted = jnp.concatenate([jnp.zeros_like(lax.slice_in_dim(array_in, 0, 1, axis=along_axis)), lax.slice_in_dim(array_in, 0, length - 1, axis=along_axis)], axis=along_axis)
    return array_in - shifted


def curl_ahead(e_field):
    ahead_xy = ahead_diff(e_field[:, 0:2], 2)
    curl_x = ahead_diff(e_field[:, 2], 3) - ahead_xy[:, 1]
    curl_y = ahead_xy[:, 0] - ahead_diff(e_field[:, 2], 2)
    curl_z = ahead_diff(e_field[:, 1], 2) - ahead_diff(e_field[:, 0], 3)
    return jnp.stack([curl_x, curl_y, curl_z], axis=1)


def curl_behind(h_field):
    behind_xy = behind_diff(h_field[:, 0:2], 2)
    curl_x = behind_diff(h_field[:, 2], 3) - behind_xy[:, 1]
    curl_y = behind_xy[:, 0] - behind_diff(h_field[:, 2], 2)
    curl_z = behind_diff(h_field[:, 1], 2) - behind_diff(h_field[:, 0], 3)
    return jnp.stack([curl_x, curl_y, curl_z], axis=1)


def smooth_axis(array_in, along_axis):
    length = array_in.shape[along_axis]
    widths = [(0, 0)] * array_in.ndim
    widths[along_axis] = (2, 2)
    padded = jnp.pad(array_in, widths)
    summed = FILTER_TAPS[0] * lax.slice_in_dim(padded, 0, length, axis=along_axis)
    for offset in range(1, 5):
        summed = summed + FILTER_TAPS[offset] * lax.slice_in_dim(padded, offset, offset + length, axis=along_axis)
    return summed


def reference(fields, spectra, inv_eps, step_phase):
    first_plane = (NZ - DZ) // 2

    def one_angle(angle_data):
        field_set, spectrum_set = angle_data
        e_field = field_set[:, 0]
        h_field = field_set[:, 1]
        re_part = spectrum_set[:, 0]
        im_part = spectrum_set[:, 1]
        for step_index in range(STEPS):
            h_field = h_field - COURANT * curl_ahead(e_field)
            e_field = e_field + COURANT * inv_eps * curl_behind(h_field)
            re_part = re_part + e_field * jnp.cos(step_phase[step_index])
            im_part = im_part + e_field * jnp.sin(step_phase[step_index])
        density = jnp.sum(re_part[0] * re_part[1] - im_part[0] * im_part[1], axis=0)
        design = lax.slice_in_dim(density, first_plane, first_plane + DZ, axis=0)
        return jnp.stack([e_field, h_field], axis=1), jnp.stack([re_part, im_part], axis=1), design

    fields_out, spectra_out, designs = lax.map(one_angle, (fields, spectra))
    mean_grad = jnp.sum(designs, axis=0) * (1.0 / ANGLES)
    symmetric = 0.5 * (mean_grad + mean_grad[:, ::-1, :])
    gradient = smooth_axis(smooth_axis(symmetric, 1), 2)
    return fields_out, spectra_out, gradient
```

```python
import functools

import jax
import jax.numpy as jnp
from jax import lax
from jax.experimental import pallas as pl
from jax.experimental.pallas import tpu as pltpu
from jax.sharding import PartitionSpec as P

MESH = pl.DeviceIdType.MESH
F32 = jnp.float32
N = 128
NP = 4
PAD = 136
R = 32
TAPS = (0.375, 0.25, 0.0625)


def lane_index(rows):
    return lax.broadcasted_iota(jnp.int32, (rows, N), 1)


def next_y(v):
    return jnp.where(lane_index(v.shape[0]) < N - 1, pltpu.roll(v, N - 1, 1), 0.0)


def prev_y(v):
    return jnp.where(lane_index(v.shape[0]) > 0, pltpu.roll(v, 1, 1), 0.0)


def chunks(body):
    def step(i, carry):
        body(pl.multiple_of(i * R, R))
        return carry

    lax.fori_loop(0, N // R, step, 0)


def filter_matrix(mirror):
    row = lax.broadcasted_iota(jnp.int32, (N, N), 0)
    col = lax.broadcasted_iota(jnp.int32, (N, N), 1)

    def taps(distance):
        out = jnp.zeros((N, N), F32)
        for k, tap in enumerate(TAPS):
            out = jnp.where(jnp.abs(distance) == k, tap, out)
        return out

    out = taps(row - col)
    if mirror:
        out = out + taps(row - (N - 1 - col))
    return out


def three_parts(v):
    high = v.astype(jnp.bfloat16)
    rest = v - high.astype(F32)
    mid = rest.astype(jnp.bfloat16)
    low = (rest - mid.astype(F32)).astype(jnp.bfloat16)
    return high, mid, low


def kernel(ns, na, f, sp, ie, ph, fo, so, g, E, H, k, e0h, keep, dz, p1s, p2s, qs, p1r, p2r, qr,
           epsu, epsl, gbuf, r1, r2, in_sem, dn_s, dn_r, up_s, up_r, g1_s, g1_r, g2_s, g2_r):
    slab = lax.axis_index("slab")
    ang = lax.axis_index("angle")
    cols = N // ns
    lo_design, hi_design = ns // 2 - 1, ns // 2
    has_below, has_above = slab > 0, slab < ns - 1
    is_design = jnp.logical_or(slab == lo_design, slab == hi_design)
    below, above = (slab - 1, ang), (slab + 1, ang)
    bar = pltpu.get_barrier_semaphore()

    def signal(device):
        pl.semaphore_signal(bar, inc=1, device_id=device, device_id_type=MESH)

    pl.when(has_below)(lambda: signal(below))
    pl.when(has_above)(lambda: signal(above))
    for d in (lo_design, hi_design):
        pl.when(slab != d)(functools.partial(signal, (d, ang)))
    for j in range(1, na):
        signal((slab, lax.rem(ang + j, na)))

    loads = []
    for s in range(2):
        loads.append(pltpu.make_async_copy(f.at[0, s, 0], E.at[s, :, 0:NP, 0:N], in_sem.at[4 * s]))
        loads.append(pltpu.make_async_copy(f.at[0, s, 1], H.at[s, :, 1 : NP + 1, 8:PAD], in_sem.at[4 * s + 1]))
        loads.append(pltpu.make_async_copy(f.at[0, s, 0, 0:2, 0], keep.at[s, :, 8:PAD], in_sem.at[4 * s + 2]))
        loads.append(pltpu.make_async_copy(sp.at[0, s], so.at[0, s], in_sem.at[4 * s + 3]))
    load_eps = pltpu.make_async_copy(ie, k, in_sem.at[8])
    for i in (0, 1):
        loads[i].start()
    load_eps.start()
    for i in (2, 4, 5, 6, 3, 7):
        loads[i].start()

    for s in range(2):
        for c in range(3):
            for z in range(NP):
                E[s, c, z, N:PAD] = jnp.zeros((PAD - N, N), F32)
                H[s, c, z + 1, 0:8] = jnp.zeros((8, N), F32)
        for c in range(2):
            e0h[s, c, 0:8] = jnp.zeros((8, N), F32)
            keep[s, c, 0:8] = jnp.zeros((8, N), F32)
        dz[s, N:PAD] = jnp.zeros((PAD - N, N), F32)

    @pl.when(slab == 0)
    def _():
        p1r[...] = jnp.zeros_like(p1r)
        p2r[...] = jnp.zeros_like(p2r)
        epsl[...] = jnp.zeros_like(epsl)

    @pl.when(slab == ns - 1)
    def _():
        e0h[...] = jnp.zeros_like(e0h)
        qr[...] = jnp.zeros_like(qr)
        epsu[...] = jnp.zeros_like(epsu)

    def down(i, src, dst):
        return pltpu.make_async_remote_copy(
            src_ref=src, dst_ref=dst, send_sem=dn_s.at[i], recv_sem=dn_r.at[i], device_id=below, device_id_type=MESH)

    def up(i, src, dst):
        return pltpu.make_async_remote_copy(
            src_ref=src, dst_ref=dst, send_sem=up_s.at[i], recv_sem=up_r.at[i], device_id=above, device_id_type=MESH)

    down_eps = down(4, ie.at[0], epsu)
    up_eps = up(4, ie.at[NP - 1], epsl)
    down_e0 = [down(s, f.at[0, s, 0, 0:2, 0], e0h.at[s, :, 8:PAD]) for s in range(2)]
    down_q = [down(2 + s, qs.at[s], qr.at[s]) for s in range(2)]
    up_p1 = [up(s, p1s.at[s], p1r.at[s]) for s in range(2)]
    up_p2 = [up(2 + s, p2s.at[s], p2r.at[s]) for s in range(2)]
    downs = [down_eps] + down_e0 + down_q
    ups = [up_eps] + up_p1 + up_p2

    def h_new(s, z, r, top):
        rows, ahead = pl.ds(r, R), pl.ds(r + 1, R)
        ex, ey, ez = (E[s, c, z, rows] for c in range(3))
        if top:
            dzx, dzy = -ex, -ey
        else:
            dzx, dzy = E[s, 0, z + 1, rows] - ex, E[s, 1, z + 1, rows] - ey
        hx, hy, hz = (H[s, c, z + 1, pl.ds(r + 8, R)] for c in range(3))
        hx = hx - 0.5 * ((next_y(ez) - ez) - dzy)
        hy = hy - 0.5 * (dzx - (E[s, 2, z, ahead] - ez))
        hz = hz - 0.5 * ((E[s, 1, z, ahead] - ey) - (next_y(ex) - ex))
        return hx, hy, hz

    def e_new(s, z, r, bottom):
        rows, behind = pl.ds(r + 8, R), pl.ds(r + 7, R)
        hx, hy, hz = (H[s, c, z + 1, rows] for c in range(3))
        if bottom:
            dzx, dzy = hx, hy
        else:
            dzx, dzy = hx - H[s, 0, z, rows], hy - H[s, 1, z, rows]
        kk = 0.5 * k[z, pl.ds(r, R)]
        old = tuple(E[s, c, z, pl.ds(r, R)] for c in range(3))
        ex = old[0] + kk * ((hz - prev_y(hz)) - dzy)
        ey = old[1] + kk * (dzx - (hz - H[s, 2, z + 1, behind]))
        ez = old[2] + kk * ((hy - H[s, 1, z + 1, behind]) - (hx - prev_y(hx)))
        return old, (ex, ey, ez)

    def first_step(s):
        def h_step(r):
            for z in range(NP):
                new = h_new(s, z, r, z == NP - 1)
                for c in range(3):
                    H[s, c, z + 1, pl.ds(r + 8, R)] = new[c]
                if z == NP - 1:
                    p1s[s, 0, pl.ds(r, R)] = new[0]
                    p1s[s, 1, pl.ds(r, R)] = new[1]

        chunks(h_step)

        def e_step(r):
            for z in range(NP):
                _, new = e_new(s, z, r, z == 0)
                for c in range(3):
                    E[s, c, z, pl.ds(r, R)] = new[c]
                if z == 0:
                    qs[s, 0, pl.ds(r, R)] = new[0]
                    qs[s, 1, pl.ds(r, R)] = new[1]

        chunks(e_step)

        def h_ahead(r):
            new = h_new(s, NP - 1, r, True)
            p2s[s, 0, pl.ds(r, R)] = new[0]
            p2s[s, 1, pl.ds(r, R)] = new[1]

        chunks(h_ahead)

    edge = jnp.where(has_below, 0.5, 0.0).astype(F32)

    def corrections(s):
        def spread(r):
            rows, behind = pl.ds(r + 8, R), pl.ds(r + 7, R)
            dx, dy = edge * keep[s, 1, rows], -edge * keep[s, 0, rows]
            kl = 0.5 * epsl[pl.ds(r, R)]
            dz[s, pl.ds(r, R)] = kl * ((dy + edge * keep[s, 0, behind]) - (dx - prev_y(dx)))

        chunks(spread)

        def fix(r):
            mid, rows, behind, ahead = pl.ds(r, R), pl.ds(r + 8, R), pl.ds(r + 7, R), pl.ds(r + 1, R)
            dx, dy = 0.5 * e0h[s, 1, rows], -0.5 * e0h[s, 0, rows]
            hx, hy = H[s, 0, NP, rows] + dx, H[s, 1, NP, rows] + dy
            H[s, 0, NP, rows] = hx
            H[s, 1, NP, rows] = hy
            k3 = 0.5 * k[NP - 1, mid]
            E[s, 0, NP - 1, mid] = E[s, 0, NP - 1, mid] - k3 * dy
            E[s, 1, NP - 1, mid] = E[s, 1, NP - 1, mid] + k3 * dx
            E[s, 2, NP - 1, mid] = E[s, 2, NP - 1, mid] + k3 * (
                (dy + 0.5 * e0h[s, 0, behind]) - (dx - prev_y(dx)))
            ku = 0.5 * epsu[mid]
            E[s, 0, NP, mid] = qr[s, 0, mid] + ku * hy
            E[s, 1, NP, mid] = qr[s, 1, mid] - ku * hx
            dx, dy = edge * keep[s, 1, rows], -edge * keep[s, 0, rows]
            k0, kl = 0.5 * k[0, mid], 0.5 * epsl[mid]
            ex = E[s, 0, 0, mid] + k0 * (p1r[s, 1, mid] + dy)
            ey = E[s, 1, 0, mid] - k0 * (p1r[s, 0, mid] + dx)
            E[s, 0, 0, mid] = ex
            E[s, 1, 0, mid] = ey
            d = dz[s, mid]
            H[s, 0, 0, rows] = p2r[s, 0, mid] + dx - 0.5 * (next_y(d) - d) + (edge * ey - 0.5 * kl * dx)
            H[s, 1, 0, rows] = p2r[s, 1, mid] + dy + 0.5 * (dz[s, ahead] - d) - (edge * ex + 0.5 * kl * dy)

        chunks(fix)

    def second_step(s):
        def h_step(r):
            for z in range(NP):
                new = h_new(s, z, r, False)
                for c in range(3):
                    H[s, c, z + 1, pl.ds(r + 8, R)] = new[c]
                    fo[0, s, 1, c, z, pl.ds(r, R)] = new[c]

        chunks(h_step)

        c0, s0, c1, s1 = (op(jnp.full((1, N), ph[t], F32)) for t in range(2) for op in (jnp.cos, jnp.sin))

        def e_step(r):
            for z in range(NP):
                old, new = e_new(s, z, r, False)
                for c in range(3):
                    rows = pl.ds(r, R)
                    fo[0, s, 0, c, z, rows] = new[c]
                    so[0, s, 0, c, z, rows] = so[0, s, 0, c, z, rows] + old[c] * c0 + new[c] * c1
                    so[0, s, 1, c, z, rows] = so[0, s, 1, c, z, rows] + old[c] * s0 + new[c] * s1

        chunks(e_step)

    loads[0].wait()
    loads[1].wait()
    load_eps.wait()
    first_step(0)
    incoming = (na - 1) + jnp.where(has_below, 1, 0) + jnp.where(has_above, 1, 0) + jnp.where(is_design, ns - 1, 0)
    pl.semaphore_wait(bar, incoming)

    @pl.when(has_below)
    def _():
        down_eps.start()
        down_e0[0].start()
        down_q[0].start()
        down_e0[1].start()

    @pl.when(has_above)
    def _():
        up_eps.start()
        up_p1[0].start()
        up_p2[0].start()

    loads[4].wait()
    loads[5].wait()
    first_step(1)
    pl.when(has_below)(lambda: down_q[1].start())

    @pl.when(has_above)
    def _():
        up_p1[1].start()
        up_p2[1].start()

    for i in (2, 6, 3, 7):
        loads[i].wait()

    for s in range(2):
        @pl.when(has_above)
        def _():
            if s == 0:
                down_eps.wait_recv()
            down_e0[s].wait_recv()
            down_q[s].wait_recv()

        @pl.when(has_below)
        def _():
            if s == 0:
                up_eps.wait_recv()
            up_p1[s].wait_recv()
            up_p2[s].wait_recv()

        corrections(s)
        second_step(s)

    def to_owner(side, owner):
        return pltpu.make_async_remote_copy(
            src_ref=gbuf.at[:, pl.ds(owner * cols, cols)], dst_ref=r1.at[pl.ds(side * NP, NP)],
            send_sem=g1_s.at[owner], recv_sem=g1_r.at[side], device_id=(owner, ang), device_id_type=MESH)

    @pl.when(is_design)
    def _():
        fy = filter_matrix(False).astype(jnp.bfloat16)
        mx = (filter_matrix(True) * (0.5 / na)).astype(jnp.bfloat16)

        def plane(z, carry):
            total = jnp.zeros((N, N), F32)
            for c in range(3):
                total = total + so[0, 0, 0, c, z] * so[0, 1, 0, c, z] - so[0, 0, 1, c, z] * so[0, 1, 1, c, z]
            along_y = sum(jnp.dot(p, fy, preferred_element_type=F32) for p in three_parts(total))
            gbuf[z] = sum(jnp.dot(mx, p, preferred_element_type=F32) for p in three_parts(along_y))
            return carry

        lax.fori_loop(0, NP, plane, 0)

    for side, d in enumerate((lo_design, hi_design)):
        @pl.when(slab == d)
        def _():
            for owner in range(ns):
                if owner != d:
                    to_owner(side, owner).start()
            r1[side * NP : (side + 1) * NP] = gbuf[:, d * cols : (d + 1) * cols]

    for side, d in enumerate((lo_design, hi_design)):
        pl.when(slab != d)(lambda: to_owner(side, slab).wait_recv())

    def to_peer(j):
        return pltpu.make_async_remote_copy(
            src_ref=r1, dst_ref=r2.at[ang], send_sem=g2_s.at[j], recv_sem=g2_r.at[ang],
            device_id=(slab, lax.rem(ang + j, na)), device_id_type=MESH)

    def from_peer(j):
        other = lax.rem(ang + j, na)
        return pltpu.make_async_remote_copy(
            src_ref=r1, dst_ref=r2.at[other], send_sem=g2_s.at[j], recv_sem=g2_r.at[other],
            device_id=(slab, other), device_id_type=MESH)

    for j in range(1, na):
        to_peer(j).start()
    r2[ang] = r1[...]
    for j in range(1, na):
        from_peer(j).wait_recv()
    total = r2[0]
    for j in range(1, na):
        total = total + r2[j]
    g[...] = total

    for j in range(1, na):
        to_peer(j).wait_send()

    @pl.when(has_below)
    def _():
        for c in downs:
            c.wait_send()

    @pl.when(has_above)
    def _():
        for c in ups:
            c.wait_send()

    for side, d in enumerate((lo_design, hi_design)):
        @pl.when(slab == d)
        def _():
            for owner in range(ns):
                if owner != d:
                    to_owner(side, owner).wait_send()


def write_out(a, b, c, x, y, z, sem):
    copies = [pltpu.make_async_copy(p, q, sem.at[i]) for i, (p, q) in enumerate(((a, x), (b, y), (c, z)))]
    for copy in copies:
        copy.start()
    for copy in copies:
        copy.wait()


def per_device(fields, spectra, inv_eps, step_phase):
    ns, na = lax.axis_size("slab"), lax.axis_size("angle")
    cols = N // ns
    shape = fields.shape
    grad = (2 * NP, cols, N)
    vmem = pl.BlockSpec(memory_space=pltpu.VMEM)
    hbm = pl.BlockSpec(memory_space=pltpu.HBM)
    outs = (shape, shape, grad)
    dma = pltpu.SemaphoreType.DMA
    planes = pltpu.VMEM((2, 2, N, N), F32)
    results = pl.pallas_call(
        functools.partial(kernel, ns, na),
        out_shape=[pltpu.VMEM(s, F32) for s in outs],
        in_specs=[hbm, hbm, hbm, pl.BlockSpec(memory_space=pltpu.SMEM)],
        out_specs=[vmem] * 3,
        scratch_shapes=[
            pltpu.VMEM((2, 3, NP + 1, PAD, N), F32),
            pltpu.VMEM((2, 3, NP + 1, PAD, N), F32),
            pltpu.VMEM((NP, N, N), F32),
            pltpu.VMEM((2, 2, PAD, N), F32),
            pltpu.VMEM((2, 2, PAD, N), F32),
            pltpu.VMEM((2, PAD, N), F32),
            planes, planes, planes, planes, planes, planes,
            pltpu.VMEM((N, N), F32),
            pltpu.VMEM((N, N), F32),
            pltpu.VMEM((NP, N, N), F32),
            pltpu.VMEM(grad, F32),
            pltpu.VMEM((na,) + grad, F32),
            dma((9,)), dma((5,)), dma((5,)), dma((5,)), dma((5,)),
            dma((ns,)), dma((2,)), dma((na,)), dma((na,)),
        ],
        compiler_params=pltpu.CompilerParams(
            collective_id=0, has_side_effects=True, vmem_limit_bytes=48 * 2**20),
        name="steps",
    )(fields, spectra, inv_eps, step_phase)
    return tuple(pl.pallas_call(
        write_out,
        out_shape=[jax.ShapeDtypeStruct(s, F32) for s in outs],
        in_specs=[vmem] * 3,
        out_specs=[pl.BlockSpec(memory_space=pl.ANY)] * 3,
        scratch_shapes=[dma((3,))],
        compiler_params=pltpu.CompilerParams(has_side_effects=True, vmem_limit_bytes=2**20),
        name="write_out",
    )(*(pltpu.with_memory_space_constraint(r, pltpu.VMEM) for r in results)))


def solution(mesh):
    cells = P("angle", None, None, None, "slab", None, None)
    return jax.shard_map(
        per_device,
        mesh=mesh,
        in_specs=(cells, cells, P("slab", None, None), P()),
        out_specs=(cells, cells, P(None, "slab", None)),
        check_vma=False,
    )
```

```python
import functools

import jax
import jax.numpy as jnp
from jax import lax
from jax.experimental import pallas as pl
from jax.experimental.pallas import tpu as pltpu
from jax.sharding import PartitionSpec as P

MESH = pl.DeviceIdType.MESH
F32 = jnp.float32
N = 128
NP = 4
PAD = 136
R = 32
TAPS = (0.375, 0.25, 0.0625)


def lane_index(rows):
    return lax.broadcasted_iota(jnp.int32, (rows, N), 1)


def next_y(v):
    return jnp.where(lane_index(v.shape[0]) < N - 1, pltpu.roll(v, N - 1, 1), 0.0)


def prev_y(v):
    return jnp.where(lane_index(v.shape[0]) > 0, pltpu.roll(v, 1, 1), 0.0)


def chunks(body):
    def step(i, carry):
        body(pl.multiple_of(i * R, R))
        return carry

    lax.fori_loop(0, N // R, step, 0)


def filter_matrix(mirror):
    row = lax.broadcasted_iota(jnp.int32, (N, N), 0)
    col = lax.broadcasted_iota(jnp.int32, (N, N), 1)

    def taps(distance):
        out = jnp.zeros((N, N), F32)
        for k, tap in enumerate(TAPS):
            out = jnp.where(jnp.abs(distance) == k, tap, out)
        return out

    out = taps(row - col)
    if mirror:
        out = out + taps(row - (N - 1 - col))
    return out


def three_parts(v):
    high = v.astype(jnp.bfloat16)
    rest = v - high.astype(F32)
    mid = rest.astype(jnp.bfloat16)
    low = (rest - mid.astype(F32)).astype(jnp.bfloat16)
    return high, mid, low


def kernel(ns, na, f, sp, ie, ph, fo, so, g, E, H, k, e0h, keep, dz, p1s, p2s, qs, p1r, p2r, qr,
           epsu, epsl, dens, fy, mx, gbuf, r1, r2, rb, in_sem, dn_s, dn_r, up_s, up_r, g1_s, g1_r, g2_s, g2_r, rl_s, rl_r):
    slab = lax.axis_index("slab")
    ang = lax.axis_index("angle")
    cols = N // ns
    lo_design, hi_design = ns // 2 - 1, ns // 2
    has_below, has_above = slab > 0, slab < ns - 1
    is_design = jnp.logical_or(slab == lo_design, slab == hi_design)
    below, above = (slab - 1, ang), (slab + 1, ang)
    relay_up, relay_down = 1, ns - 1
    bar = pltpu.get_barrier_semaphore()

    def signal(device):
        pl.semaphore_signal(bar, inc=1, device_id=device, device_id_type=MESH)

    pl.when(has_below)(lambda: signal(below))
    pl.when(has_above)(lambda: signal(above))
    for d in (lo_design, hi_design):
        pl.when(slab != d)(functools.partial(signal, (d, ang)))
    pl.when(slab == hi_design)(lambda: signal((relay_up, ang)))
    pl.when(slab == lo_design)(lambda: signal((relay_down, ang)))
    for j in range(1, na):
        signal((slab, lax.rem(ang + j, na)))

    loads = []
    for s in range(2):
        loads.append(pltpu.make_async_copy(f.at[0, s, 0], E.at[s, :, 0:NP, 0:N], in_sem.at[4 * s]))
        loads.append(pltpu.make_async_copy(f.at[0, s, 1], H.at[s, :, 1 : NP + 1, 8:PAD], in_sem.at[4 * s + 1]))
        loads.append(pltpu.make_async_copy(f.at[0, s, 0, 0:2, 0], keep.at[s, :, 8:PAD], in_sem.at[4 * s + 2]))
        loads.append(pltpu.make_async_copy(sp.at[0, s], so.at[0, s], in_sem.at[4 * s + 3]))
    load_eps = pltpu.make_async_copy(ie, k, in_sem.at[8])
    for i in (0, 1):
        loads[i].start()
    load_eps.start()
    for i in (2, 4, 5, 6, 3, 7):
        loads[i].start()

    for s in range(2):
        for c in range(3):
            for z in range(NP):
                E[s, c, z, N:PAD] = jnp.zeros((PAD - N, N), F32)
                H[s, c, z + 1, 0:8] = jnp.zeros((8, N), F32)
        for c in range(2):
            e0h[s, c, 0:8] = jnp.zeros((8, N), F32)
            keep[s, c, 0:8] = jnp.zeros((8, N), F32)
        dz[s, N:PAD] = jnp.zeros((PAD - N, N), F32)

    @pl.when(slab == 0)
    def _():
        p1r[...] = jnp.zeros_like(p1r)
        p2r[...] = jnp.zeros_like(p2r)
        epsl[...] = jnp.zeros_like(epsl)

    @pl.when(slab == ns - 1)
    def _():
        e0h[...] = jnp.zeros_like(e0h)
        qr[...] = jnp.zeros_like(qr)
        epsu[...] = jnp.zeros_like(epsu)

    def down(i, src, dst):
        return pltpu.make_async_remote_copy(
            src_ref=src, dst_ref=dst, send_sem=dn_s.at[i], recv_sem=dn_r.at[i], device_id=below, device_id_type=MESH)

    def up(i, src, dst):
        return pltpu.make_async_remote_copy(
            src_ref=src, dst_ref=dst, send_sem=up_s.at[i], recv_sem=up_r.at[i], device_id=above, device_id_type=MESH)

    down_eps = down(4, ie.at[0], epsu)
    up_eps = up(4, ie.at[NP - 1], epsl)
    down_e0 = [down(s, f.at[0, s, 0, 0:2, 0], e0h.at[s, :, 8:PAD]) for s in range(2)]
    down_q = [down(2 + s, qs.at[s], qr.at[s]) for s in range(2)]
    up_p1 = [up(s, p1s.at[s], p1r.at[s]) for s in range(2)]
    up_p2 = [up(2 + s, p2s.at[s], p2r.at[s]) for s in range(2)]
    def relayed(s, c, src, device):
        return pltpu.make_async_remote_copy(
            src_ref=src.at[s, c], dst_ref=rb.at[s, c], send_sem=rl_s.at[2 * s + c], recv_sem=rl_r.at[2 * s + c],
            device_id=(device, ang), device_id_type=MESH)

    def passed_on(s, c, dst, sems, device):
        return pltpu.make_async_remote_copy(
            src_ref=rb.at[s, c], dst_ref=dst.at[s, c], send_sem=rl_s.at[2 * s + c], recv_sem=sems.at[2 + s],
            device_id=(device, ang), device_id_type=MESH)

    def send_q(s):
        pl.when(jnp.logical_and(has_below, slab != hi_design))(lambda: down_q[s].start())

        @pl.when(slab == hi_design)
        def _():
            for c in range(2):
                relayed(s, c, qs, relay_down).start()

    def send_p2(s):
        pl.when(jnp.logical_and(has_above, slab != lo_design))(lambda: up_p2[s].start())

        @pl.when(slab == lo_design)
        def _():
            for c in range(2):
                relayed(s, c, p2s, relay_up).start()

    def pass_on(s):
        for relay, src, dst, sems, device in (
            (relay_up, p2s, p2r, up_r, hi_design), (relay_down, qs, qr, dn_r, lo_design)):
            @pl.when(slab == relay)
            def _():
                for c in range(2):
                    relayed(s, c, src, relay).wait_recv()
                    passed_on(s, c, dst, sems, device).start()

    def h_new(s, z, r, top):
        rows, ahead = pl.ds(r, R), pl.ds(r + 1, R)
        ex, ey, ez = (E[s, c, z, rows] for c in range(3))
        if top:
            dzx, dzy = -ex, -ey
        else:
            dzx, dzy = E[s, 0, z + 1, rows] - ex, E[s, 1, z + 1, rows] - ey
        hx, hy, hz = (H[s, c, z + 1, pl.ds(r + 8, R)] for c in range(3))
        hx = hx - 0.5 * ((next_y(ez) - ez) - dzy)
        hy = hy - 0.5 * (dzx - (E[s, 2, z, ahead] - ez))
        hz = hz - 0.5 * ((E[s, 1, z, ahead] - ey) - (next_y(ex) - ex))
        return hx, hy, hz

    def e_new(s, z, r, bottom):
        rows, behind = pl.ds(r + 8, R), pl.ds(r + 7, R)
        hx, hy, hz = (H[s, c, z + 1, rows] for c in range(3))
        if bottom:
            dzx, dzy = hx, hy
        else:
            dzx, dzy = hx - H[s, 0, z, rows], hy - H[s, 1, z, rows]
        kk = 0.5 * k[z, pl.ds(r, R)]
        old = tuple(E[s, c, z, pl.ds(r, R)] for c in range(3))
        ex = old[0] + kk * ((hz - prev_y(hz)) - dzy)
        ey = old[1] + kk * (dzx - (hz - H[s, 2, z + 1, behind]))
        ez = old[2] + kk * ((hy - H[s, 1, z + 1, behind]) - (hx - prev_y(hx)))
        return old, (ex, ey, ez)

    def first_step(s):
        def h_step(r):
            for z in range(NP):
                new = h_new(s, z, r, z == NP - 1)
                for c in range(3):
                    H[s, c, z + 1, pl.ds(r + 8, R)] = new[c]
                if z == NP - 1:
                    p1s[s, 0, pl.ds(r, R)] = new[0]
                    p1s[s, 1, pl.ds(r, R)] = new[1]

        chunks(h_step)

        def e_step(r):
            for z in range(NP):
                _, new = e_new(s, z, r, z == 0)
                for c in range(3):
                    E[s, c, z, pl.ds(r, R)] = new[c]
                if z == 0:
                    qs[s, 0, pl.ds(r, R)] = new[0]
                    qs[s, 1, pl.ds(r, R)] = new[1]

        chunks(e_step)

        def h_ahead(r):
            new = h_new(s, NP - 1, r, True)
            p2s[s, 0, pl.ds(r, R)] = new[0]
            p2s[s, 1, pl.ds(r, R)] = new[1]

        chunks(h_ahead)

    edge = jnp.where(has_below, 0.5, 0.0).astype(F32)

    def fix_above(s):
        def fix(r):
            mid, rows, behind = pl.ds(r, R), pl.ds(r + 8, R), pl.ds(r + 7, R)
            dx, dy = 0.5 * e0h[s, 1, rows], -0.5 * e0h[s, 0, rows]
            hx, hy = H[s, 0, NP, rows] + dx, H[s, 1, NP, rows] + dy
            H[s, 0, NP, rows] = hx
            H[s, 1, NP, rows] = hy
            k3 = 0.5 * k[NP - 1, mid]
            E[s, 0, NP - 1, mid] = E[s, 0, NP - 1, mid] - k3 * dy
            E[s, 1, NP - 1, mid] = E[s, 1, NP - 1, mid] + k3 * dx
            E[s, 2, NP - 1, mid] = E[s, 2, NP - 1, mid] + k3 * (
                (dy + 0.5 * e0h[s, 0, behind]) - (dx - prev_y(dx)))
            ku = 0.5 * epsu[mid]
            E[s, 0, NP, mid] = qr[s, 0, mid] + ku * hy
            E[s, 1, NP, mid] = qr[s, 1, mid] - ku * hx

        chunks(fix)

    def fix_below(s):
        def spread(r):
            rows, behind = pl.ds(r + 8, R), pl.ds(r + 7, R)
            dx, dy = edge * keep[s, 1, rows], -edge * keep[s, 0, rows]
            kl = 0.5 * epsl[pl.ds(r, R)]
            dz[s, pl.ds(r, R)] = kl * ((dy + edge * keep[s, 0, behind]) - (dx - prev_y(dx)))

        chunks(spread)

        def fix(r):
            mid, rows, ahead = pl.ds(r, R), pl.ds(r + 8, R), pl.ds(r + 1, R)
            dx, dy = edge * keep[s, 1, rows], -edge * keep[s, 0, rows]
            k0, kl = 0.5 * k[0, mid], 0.5 * epsl[mid]
            ex = E[s, 0, 0, mid] + k0 * (p1r[s, 1, mid] + dy)
            ey = E[s, 1, 0, mid] - k0 * (p1r[s, 0, mid] + dx)
            E[s, 0, 0, mid] = ex
            E[s, 1, 0, mid] = ey
            d = dz[s, mid]
            H[s, 0, 0, rows] = p2r[s, 0, mid] + dx - 0.5 * (next_y(d) - d) + (edge * ey - 0.5 * kl * dx)
            H[s, 1, 0, rows] = p2r[s, 1, mid] + dy + 0.5 * (dz[s, ahead] - d) - (edge * ex + 0.5 * kl * dy)

        chunks(fix)

    def second_h(s, planes):
        def h_step(r):
            for z in planes:
                new = h_new(s, z, r, False)
                for c in range(3):
                    H[s, c, z + 1, pl.ds(r + 8, R)] = new[c]
                    fo[0, s, 1, c, z, pl.ds(r, R)] = new[c]

        chunks(h_step)

    def second_e(s, planes):
        c0, s0, c1, s1 = (op(jnp.full((1, N), ph[t], F32)) for t in range(2) for op in (jnp.cos, jnp.sin))

        def e_step(r):
            for z in planes:
                old, new = e_new(s, z, r, False)
                total = jnp.zeros((R, N), F32)
                for c in range(3):
                    rows = pl.ds(r, R)
                    fo[0, s, 0, c, z, rows] = new[c]
                    re = so[0, s, 0, c, z, rows] + old[c] * c0 + new[c] * c1
                    im = so[0, s, 1, c, z, rows] + old[c] * s0 + new[c] * s1
                    so[0, s, 0, c, z, rows] = re
                    so[0, s, 1, c, z, rows] = im
                    if s == 1:
                        total = total + so[0, 0, 0, c, z, rows] * re - so[0, 0, 1, c, z, rows] * im
                if s == 1:
                    dens[z, rows] = total

        chunks(e_step)

    def lower_planes(s):
        @pl.when(has_below)
        def _():
            if s == 0:
                up_eps.wait_recv()
            up_p1[s].wait_recv()
            up_p2[s].wait_recv()

        fix_below(s)
        second_h(s, (0,))
        second_e(s, (0, 1))

    def upper_planes(s):
        @pl.when(has_above)
        def _():
            if s == 0:
                down_eps.wait_recv()
            down_e0[s].wait_recv()
            down_q[s].wait_recv()

        fix_above(s)
        second_h(s, (2, 3))
        second_e(s, (2, 3))

    loads[0].wait()
    loads[1].wait()
    load_eps.wait()
    first_step(0)
    incoming = (na - 1) + jnp.where(has_below, 1, 0) + jnp.where(has_above, 1, 0) + jnp.where(is_design, ns - 1, 0)
    incoming = incoming + jnp.where(jnp.logical_or(slab == relay_up, slab == relay_down), 1, 0)
    pl.semaphore_wait(bar, incoming)

    @pl.when(has_below)
    def _():
        down_eps.start()
        down_e0[0].start()
        down_e0[1].start()

    @pl.when(has_above)
    def _():
        up_eps.start()
        up_p1[0].start()

    send_q(0)
    send_p2(0)
    loads[4].wait()
    loads[5].wait()
    first_step(1)
    pl.when(has_above)(lambda: up_p1[1].start())
    send_q(1)
    send_p2(1)
    for s in range(2):
        pass_on(s)
    for s in range(2):
        second_h(s, (1,))
    fy[...] = filter_matrix(False).astype(jnp.bfloat16)
    mx[...] = (filter_matrix(True) * (0.5 / na)).astype(jnp.bfloat16)
    for i in (2, 6, 3, 7):
        loads[i].wait()

    half = NP // 2

    def to_owner(part, side, owner):
        return pltpu.make_async_remote_copy(
            src_ref=gbuf.at[part, :, pl.ds(owner * cols, cols)], dst_ref=r1.at[part, pl.ds(side * half, half)],
            send_sem=g1_s.at[part, owner], recv_sem=g1_r.at[part, side], device_id=(owner, ang), device_id_type=MESH)

    def spread_density(part, first, side):
        planes = dens[first : first + half].reshape(half * N, N)
        along_y = sum(jnp.dot(p, fy[...], preferred_element_type=F32) for p in three_parts(planes))
        beside = jnp.concatenate([along_y[z * N : (z + 1) * N] for z in range(half)], axis=1)
        both = sum(jnp.dot(mx[...], p, preferred_element_type=F32) for p in three_parts(beside))
        for z in range(half):
            gbuf[part, z] = both[:, z * N : (z + 1) * N]
        d = (lo_design, hi_design)[side]
        for owner in range(ns):
            if owner != d:
                to_owner(part, side, owner).start()
        r1[part, side * half : (side + 1) * half] = gbuf[part, :, d * cols : (d + 1) * cols]

    second = (lower_planes, upper_planes)
    for odd in (0, 1):
        @pl.when(slab % 2 == odd)
        def _():
            design = (hi_design, lo_design)[odd]
            for part in (0, 1):
                upper = part if odd else 1 - part
                for s in range(2):
                    second[upper](s)
                pl.when(slab == design)(functools.partial(spread_density, part, half * upper, 1 - odd))

    def to_peer(part, j):
        return pltpu.make_async_remote_copy(
            src_ref=r1.at[part], dst_ref=r2.at[part, ang], send_sem=g2_s.at[part, j], recv_sem=g2_r.at[part, ang],
            device_id=(slab, lax.rem(ang + j, na)), device_id_type=MESH)

    def from_peer(part, j):
        other = lax.rem(ang + j, na)
        return pltpu.make_async_remote_copy(
            src_ref=r1.at[part], dst_ref=r2.at[part, other], send_sem=g2_s.at[part, j],
            recv_sem=g2_r.at[part, other], device_id=(slab, other), device_id_type=MESH)

    for part in (0, 1):
        for side, d in enumerate((lo_design, hi_design)):
            pl.when(slab != d)(lambda: to_owner(part, side, slab).wait_recv())
        for j in range(1, na):
            to_peer(part, j).start()
        r2[part, ang] = r1[part]
    for part in (0, 1):
        for j in range(1, na):
            from_peer(part, j).wait_recv()
        total = r2[part, 0]
        for j in range(1, na):
            total = total + r2[part, j]
        if part == 0:
            g[0:half] = total[0:half]
            g[NP + half :] = total[half:]
        else:
            g[half : NP + half] = total

    for part in (0, 1):
        for j in range(1, na):
            to_peer(part, j).wait_send()

    @pl.when(has_below)
    def _():
        for c in [down_eps] + down_e0:
            c.wait_send()

    @pl.when(has_above)
    def _():
        for c in [up_eps] + up_p1:
            c.wait_send()

    @pl.when(jnp.logical_and(has_below, slab != hi_design))
    def _():
        for c in down_q:
            c.wait_send()

    @pl.when(jnp.logical_and(has_above, slab != lo_design))
    def _():
        for c in up_p2:
            c.wait_send()

    for d, src in ((hi_design, qs), (lo_design, p2s), (relay_up, rb), (relay_down, rb)):
        @pl.when(slab == d)
        def _():
            for s in range(2):
                for c in range(2):
                    relayed(s, c, src, d).wait_send()

    for side, d in enumerate((lo_design, hi_design)):
        @pl.when(slab == d)
        def _():
            for owner in range(ns):
                if owner != d:
                    for part in (0, 1):
                        to_owner(part, side, owner).wait_send()


def write_out(a, b, c, x, y, z, sem):
    copies = [pltpu.make_async_copy(p, q, sem.at[i]) for i, (p, q) in enumerate(((a, x), (b, y), (c, z)))]
    for copy in copies:
        copy.start()
    for copy in copies:
        copy.wait()


def per_device(fields, spectra, inv_eps, step_phase):
    ns, na = lax.axis_size("slab"), lax.axis_size("angle")
    cols = N // ns
    shape = fields.shape
    grad = (2 * NP, cols, N)
    vmem = pl.BlockSpec(memory_space=pltpu.VMEM)
    hbm = pl.BlockSpec(memory_space=pltpu.HBM)
    outs = (shape, shape, grad)
    dma = pltpu.SemaphoreType.DMA
    planes = pltpu.VMEM((2, 2, N, N), F32)
    results = pl.pallas_call(
        functools.partial(kernel, ns, na),
        out_shape=[pltpu.VMEM(s, F32) for s in outs],
        in_specs=[hbm, hbm, hbm, pl.BlockSpec(memory_space=pltpu.SMEM)],
        out_specs=[vmem] * 3,
        scratch_shapes=[
            pltpu.VMEM((2, 3, NP + 1, PAD, N), F32),
            pltpu.VMEM((2, 3, NP + 1, PAD, N), F32),
            pltpu.VMEM((NP, N, N), F32),
            pltpu.VMEM((2, 2, PAD, N), F32),
            pltpu.VMEM((2, 2, PAD, N), F32),
            pltpu.VMEM((2, PAD, N), F32),
            planes, planes, planes, planes, planes, planes,
            pltpu.VMEM((N, N), F32),
            pltpu.VMEM((N, N), F32),
            pltpu.VMEM((NP, N, N), F32),
            pltpu.VMEM((N, N), jnp.bfloat16),
            pltpu.VMEM((N, N), jnp.bfloat16),
            pltpu.VMEM((2, NP // 2, N, N), F32),
            pltpu.VMEM((2, NP, cols, N), F32),
            pltpu.VMEM((2, na, NP, cols, N), F32),
            planes,
            dma((9,)), dma((5,)), dma((5,)), dma((5,)), dma((5,)),
            dma((2, ns)), dma((2, 2)), dma((2, na)), dma((2, na)), dma((4,)), dma((4,)),
        ],
        compiler_params=pltpu.CompilerParams(
            collective_id=0, has_side_effects=True, vmem_limit_bytes=48 * 2**20),
        name="steps",
    )(fields, spectra, inv_eps, step_phase)
    return tuple(pl.pallas_call(
        write_out,
        out_shape=[jax.ShapeDtypeStruct(s, F32) for s in outs],
        in_specs=[vmem] * 3,
        out_specs=[pl.BlockSpec(memory_space=pl.ANY)] * 3,
        scratch_shapes=[dma((3,))],
        compiler_params=pltpu.CompilerParams(has_side_effects=True, vmem_limit_bytes=2**20),
        name="write_out",
    )(*(pltpu.with_memory_space_constraint(r, pltpu.VMEM) for r in results)))


def solution(mesh):
    cells = P("angle", None, None, None, "slab", None, None)
    return jax.shard_map(
        per_device,
        mesh=mesh,
        in_specs=(cells, cells, P("slab", None, None), P()),
        out_specs=(cells, cells, P(None, "slab", None)),
        check_vma=False,
    )
```

```python
import functools

import jax
import jax.numpy as jnp
from jax import lax
from jax.experimental import pallas as pl
from jax.experimental.pallas import tpu as pltpu
from jax.sharding import PartitionSpec as P

MESH = pl.DeviceIdType.MESH
F32 = jnp.float32
N = 128
NP = 4
HALF = NP // 2
PAD = 136
TAPS = (0.375, 0.25, 0.0625)
E_ROWS, E_AHEAD = pl.ds(0, N), pl.ds(1, N)
H_ROWS, H_BEHIND = pl.ds(8, N), pl.ds(7, N)


def lane_index(rows):
    return lax.broadcasted_iota(jnp.int32, (rows, N), 1)


def next_y(v):
    return jnp.where(lane_index(v.shape[0]) < N - 1, pltpu.roll(v, N - 1, 1), 0.0)


def prev_y(v):
    return jnp.where(lane_index(v.shape[0]) > 0, pltpu.roll(v, 1, 1), 0.0)


def filter_matrix(mirror):
    row = lax.broadcasted_iota(jnp.int32, (N, N), 0)
    col = lax.broadcasted_iota(jnp.int32, (N, N), 1)

    def taps(distance):
        out = jnp.zeros((N, N), F32)
        for k, tap in enumerate(TAPS):
            out = jnp.where(jnp.abs(distance) == k, tap, out)
        return out

    out = taps(row - col)
    if mirror:
        out = out + taps(row - (N - 1 - col))
    return out


def three_parts(v):
    high = v.astype(jnp.bfloat16)
    rest = v - high.astype(F32)
    mid = rest.astype(jnp.bfloat16)
    low = (rest - mid.astype(F32)).astype(jnp.bfloat16)
    return high, mid, low


def kernel(ns, na, f, sp, ie, ph, fo, so, g, E, H, k, e0h, keep, dz, p1s, p2s, qs, p1r, p2r, qr,
           epsu, epsl, dens, fy, mx, gbuf, r1, r2, rb, in_sem, dn_s, dn_r, up_s, up_r, rl_s, rl_r,
           g1_s, g1_r, g2_s, g2_r):
    slab = lax.axis_index("slab")
    ang = lax.axis_index("angle")
    cols = N // ns
    lo_design, hi_design = ns // 2 - 1, ns // 2
    has_below, has_above = slab > 0, slab < ns - 1
    is_design = jnp.logical_or(slab == lo_design, slab == hi_design)
    relay_up, relay_down = 1, ns - 1
    bar = pltpu.get_barrier_semaphore()

    def signal(slab_index, angle_index):
        pl.semaphore_signal(bar, inc=1, device_id=(slab_index, angle_index), device_id_type=MESH)

    def send(src, dst, send_sem, recv_sem, slab_index, angle_index):
        return pltpu.make_async_remote_copy(
            src_ref=src, dst_ref=dst, send_sem=send_sem, recv_sem=recv_sem,
            device_id=(slab_index, angle_index), device_id_type=MESH)

    def wait_bytes(ref, sem):
        pltpu.make_async_copy(ref, ref, sem).wait()

    pl.when(has_below)(lambda: signal(slab - 1, ang))
    pl.when(has_above)(lambda: signal(slab + 1, ang))
    for d in (lo_design, hi_design):
        pl.when(slab != d)(functools.partial(signal, d, ang))
    pl.when(slab == hi_design)(lambda: signal(relay_up, ang))
    pl.when(slab == lo_design)(lambda: signal(relay_down, ang))
    for j in range(1, na):
        signal(slab, lax.rem(ang + j, na))

    for s in range(2):
        pltpu.make_async_copy(f.at[0, s, 0], E.at[s, :, 0:NP, E_ROWS], in_sem.at[s]).start()
        pltpu.make_async_copy(f.at[0, s, 1], H.at[s, :, 1 : NP + 1, H_ROWS], in_sem.at[s]).start()
        if s == 0:
            load_eps = pltpu.make_async_copy(ie, k, in_sem.at[2])
            load_eps.start()
    load_keep = pltpu.make_async_copy(f.at[0, :, 0, 0:2, 0], keep.at[:, :, H_ROWS], in_sem.at[3])
    load_keep.start()
    load_spectra = pltpu.make_async_copy(sp, so, in_sem.at[4])
    load_spectra.start()

    for s in range(2):
        for c in range(3):
            for z in range(NP):
                E[s, c, z, N:PAD] = jnp.zeros((PAD - N, N), F32)
                H[s, c, z + 1, 0:8] = jnp.zeros((8, N), F32)
        for c in range(2):
            e0h[s, c, 0:8] = jnp.zeros((8, N), F32)
            keep[s, c, 0:8] = jnp.zeros((8, N), F32)
    dz[N:PAD] = jnp.zeros((PAD - N, N), F32)

    @pl.when(slab == 0)
    def _():
        p1r[...] = jnp.zeros_like(p1r)
        p2r[...] = jnp.zeros_like(p2r)
        epsl[...] = jnp.zeros_like(epsl)

    @pl.when(slab == ns - 1)
    def _():
        e0h[...] = jnp.zeros_like(e0h)
        qr[...] = jnp.zeros_like(qr)
        epsu[...] = jnp.zeros_like(epsu)

    def down(src, dst, i):
        return send(src, dst, dn_s, dn_r.at[i], slab - 1, ang)

    def up(src, dst, i):
        return send(src, dst, up_s, up_r.at[i], slab + 1, ang)

    def send_q(s):
        pl.when(jnp.logical_and(has_below, slab != hi_design))(lambda: down(qs.at[s], qr.at[s], s).start())

        @pl.when(slab == hi_design)
        def _():
            for c in range(2):
                send(qs.at[s, c], rb.at[s, c], dn_s, rl_r.at[2 * s + c], relay_down, ang).start()

    def send_p2(s):
        pl.when(jnp.logical_and(has_above, slab != lo_design))(lambda: up(p2s.at[s], p2r.at[s], s).start())

        @pl.when(slab == lo_design)
        def _():
            for c in range(2):
                send(p2s.at[s, c], rb.at[s, c], up_s, rl_r.at[2 * s + c], relay_up, ang).start()

    def pass_on(s):
        for relay, dst, sems, d in ((relay_up, p2r, up_r, hi_design), (relay_down, qr, dn_r, lo_design)):
            @pl.when(slab == relay)
            def _():
                for c in range(2):
                    wait_bytes(rb.at[s, c], rl_r.at[2 * s + c])
                    send(rb.at[s, c], dst.at[s, c], rl_s, sems.at[s], d, ang).start()

    def h_new(s, z, top):
        ex, ey, ez = (E[s, c, z, E_ROWS] for c in range(3))
        if top:
            dzx, dzy = -ex, -ey
        else:
            dzx, dzy = E[s, 0, z + 1, E_ROWS] - ex, E[s, 1, z + 1, E_ROWS] - ey
        hx, hy, hz = (H[s, c, z + 1, H_ROWS] for c in range(3))
        hx = hx - 0.5 * ((next_y(ez) - ez) - dzy)
        hy = hy - 0.5 * (dzx - (E[s, 2, z, E_AHEAD] - ez))
        hz = hz - 0.5 * ((E[s, 1, z, E_AHEAD] - ey) - (next_y(ex) - ex))
        return hx, hy, hz

    def e_new(s, z, bottom):
        hx, hy, hz = (H[s, c, z + 1, H_ROWS] for c in range(3))
        if bottom:
            dzx, dzy = hx, hy
        else:
            dzx, dzy = hx - H[s, 0, z, H_ROWS], hy - H[s, 1, z, H_ROWS]
        kk = 0.5 * k[z]
        old = tuple(E[s, c, z, E_ROWS] for c in range(3))
        ex = old[0] + kk * ((hz - prev_y(hz)) - dzy)
        ey = old[1] + kk * (dzx - (hz - H[s, 2, z + 1, H_BEHIND]))
        ez = old[2] + kk * ((hy - H[s, 1, z + 1, H_BEHIND]) - (hx - prev_y(hx)))
        return old, (ex, ey, ez)

    def first_step(s):
        for z in range(NP):
            new = h_new(s, z, z == NP - 1)
            for c in range(3):
                H[s, c, z + 1, H_ROWS] = new[c]
        for c in range(2):
            p1s[s, c] = new[c]
        for z in range(NP):
            _, new = e_new(s, z, z == 0)
            for c in range(3):
                E[s, c, z, E_ROWS] = new[c]
                if z == 0 and c < 2:
                    qs[s, c] = new[c]
        new = h_new(s, NP - 1, True)
        for c in range(2):
            p2s[s, c] = new[c]

    edge = jnp.where(has_below, 0.5, 0.0).astype(F32)

    def fix_above(s):
        dx, dy = 0.5 * e0h[s, 1, H_ROWS], -0.5 * e0h[s, 0, H_ROWS]
        hx, hy = H[s, 0, NP, H_ROWS] + dx, H[s, 1, NP, H_ROWS] + dy
        H[s, 0, NP, H_ROWS] = hx
        H[s, 1, NP, H_ROWS] = hy
        k3 = 0.5 * k[NP - 1]
        E[s, 0, NP - 1, E_ROWS] = E[s, 0, NP - 1, E_ROWS] - k3 * dy
        E[s, 1, NP - 1, E_ROWS] = E[s, 1, NP - 1, E_ROWS] + k3 * dx
        E[s, 2, NP - 1, E_ROWS] = E[s, 2, NP - 1, E_ROWS] + k3 * (
            (dy + 0.5 * e0h[s, 0, H_BEHIND]) - (dx - prev_y(dx)))
        ku = 0.5 * epsu[...]
        E[s, 0, NP, E_ROWS] = qr[s, 0] + ku * hy
        E[s, 1, NP, E_ROWS] = qr[s, 1] - ku * hx

    def fix_below(s):
        dx, dy = edge * keep[s, 1, H_ROWS], -edge * keep[s, 0, H_ROWS]
        k0, kl = 0.5 * k[0], 0.5 * epsl[...]
        d = kl * ((dy + edge * keep[s, 0, H_BEHIND]) - (dx - prev_y(dx)))
        dz[E_ROWS] = d
        ex = E[s, 0, 0, E_ROWS] + k0 * (p1r[s, 1] + dy)
        ey = E[s, 1, 0, E_ROWS] - k0 * (p1r[s, 0] + dx)
        E[s, 0, 0, E_ROWS] = ex
        E[s, 1, 0, E_ROWS] = ey
        H[s, 0, 0, H_ROWS] = p2r[s, 0] + dx - 0.5 * (next_y(d) - d) + (edge * ey - 0.5 * kl * dx)
        H[s, 1, 0, H_ROWS] = p2r[s, 1] + dy + 0.5 * (dz[E_AHEAD] - d) - (edge * ex + 0.5 * kl * dy)

    def second_h(s, planes):
        for z in planes:
            new = h_new(s, z, False)
            for c in range(3):
                H[s, c, z + 1, H_ROWS] = new[c]
                fo[0, s, 1, c, z] = new[c]

    def second_e(s, planes):
        c0, s0, c1, s1 = (op(jnp.full((1, N), ph[t], F32)) for t in range(2) for op in (jnp.cos, jnp.sin))
        for z in planes:
            old, new = e_new(s, z, False)
            total = jnp.zeros((N, N), F32)
            for c in range(3):
                fo[0, s, 0, c, z] = new[c]
                re = so[0, s, 0, c, z] + old[c] * c0 + new[c] * c1
                im = so[0, s, 1, c, z] + old[c] * s0 + new[c] * s1
                so[0, s, 0, c, z] = re
                so[0, s, 1, c, z] = im
                if s == 1:
                    total = total + so[0, 0, 0, c, z] * re - so[0, 0, 1, c, z] * im
            if s == 1:
                dens[z] = total

    def lower_planes(s):
        @pl.when(has_below)
        def _():
            if s == 0:
                wait_bytes(epsl, up_r.at[2])
            wait_bytes(fo.at[0, s, 0, 0], up_r.at[s])

        fix_below(s)
        second_h(s, (0,))
        second_e(s, (0, 1))

    def upper_planes(s):
        @pl.when(has_above)
        def _():
            if s == 0:
                wait_bytes(epsu, dn_r.at[2])
            wait_bytes(fo.at[0, s, 0, 0], dn_r.at[s])

        fix_above(s)
        second_h(s, (2, 3))
        second_e(s, (2, 3))

    wait_bytes(so.at[0, 0], in_sem.at[0])
    load_eps.wait()
    first_step(0)
    incoming = (na - 1) + jnp.where(has_below, 1, 0) + jnp.where(has_above, 1, 0) + jnp.where(is_design, ns - 1, 0)
    incoming = incoming + jnp.where(jnp.logical_or(slab == relay_up, slab == relay_down), 1, 0)
    pl.semaphore_wait(bar, incoming)

    @pl.when(has_below)
    def _():
        down(ie.at[0], epsu, 2).start()
        for s in range(2):
            down(f.at[0, s, 0, 0:2, 0], e0h.at[s, :, H_ROWS], s).start()

    @pl.when(has_above)
    def _():
        up(ie.at[NP - 1], epsl, 2).start()
        up(p1s.at[0], p1r.at[0], 0).start()

    send_q(0)
    send_p2(0)
    wait_bytes(so.at[0, 1], in_sem.at[1])
    first_step(1)
    pl.when(has_above)(lambda: up(p1s.at[1], p1r.at[1], 1).start())
    send_q(1)
    send_p2(1)
    for s in range(2):
        pass_on(s)
    for s in range(2):
        second_h(s, (1,))
    fy[...] = filter_matrix(False).astype(jnp.bfloat16)
    mx[...] = (filter_matrix(True) * (0.5 / na)).astype(jnp.bfloat16)
    load_keep.wait()
    load_spectra.wait()

    def to_owner(part, side, owner):
        return send(gbuf.at[part, :, pl.ds(owner * cols, cols)], r1.at[part, pl.ds(side * HALF, HALF)],
                    g1_s, g1_r.at[part], owner, ang)

    def spread_density(part, first, side):
        planes = dens[first : first + HALF].reshape(HALF * N, N)
        along_y = sum(jnp.dot(p, fy[...], preferred_element_type=F32) for p in three_parts(planes))
        beside = jnp.concatenate([along_y[z * N : (z + 1) * N] for z in range(HALF)], axis=1)
        both = sum(jnp.dot(mx[...], p, preferred_element_type=F32) for p in three_parts(beside))
        for z in range(HALF):
            gbuf[part, z] = both[:, z * N : (z + 1) * N]
        d = (lo_design, hi_design)[side]
        for owner in range(ns):
            if owner != d:
                to_owner(part, side, owner).start()
        r1[part, side * HALF : (side + 1) * HALF] = gbuf[part, :, d * cols : (d + 1) * cols]

    second = (lower_planes, upper_planes)
    for odd in (0, 1):
        @pl.when(slab % 2 == odd)
        def _():
            design = (hi_design, lo_design)[odd]
            for part in (0, 1):
                upper = part if odd else 1 - part
                for s in range(2):
                    second[upper](s)
                pl.when(slab == design)(functools.partial(spread_density, part, HALF * upper, 1 - odd))

    for part in (0, 1):
        pl.when(is_design)(lambda: wait_bytes(r1.at[part, pl.ds(0, HALF)], g1_r.at[part]))
        pl.when(jnp.logical_not(is_design))(lambda: wait_bytes(r1.at[part], g1_r.at[part]))
        for j in range(1, na):
            send(r1.at[part], r2.at[part, ang], g2_s, g2_r.at[part], slab, lax.rem(ang + j, na)).start()
        r2[part, ang] = r1[part]
    for part in (0, 1):
        wait_bytes(r2.at[part, pl.ds(0, na - 1)], g2_r.at[part])
        total = r2[part, 0]
        for j in range(1, na):
            total = total + r2[part, j]
        if part == 0:
            g[0:HALF] = total[0:HALF]
            g[NP + HALF :] = total[HALF:]
        else:
            g[HALF : NP + HALF] = total

    wait_bytes(r2.at[:, pl.ds(0, na - 1)], g2_s)
    nine_planes = E.at[0, 0:3, 0:3, E_ROWS]
    pl.when(has_below)(lambda: wait_bytes(nine_planes, dn_s))
    pl.when(has_above)(lambda: wait_bytes(nine_planes, up_s))
    pl.when(jnp.logical_or(slab == relay_up, slab == relay_down))(lambda: wait_bytes(rb, rl_s))
    pl.when(is_design)(lambda: wait_bytes(gbuf.at[:, :, pl.ds(0, N - cols)], g1_s))


def write_out(a, b, c, x, y, z, sem):
    copies = [pltpu.make_async_copy(p, q, sem.at[i]) for i, (p, q) in enumerate(((a, x), (b, y), (c, z)))]
    for copy in copies:
        copy.start()
    for copy in copies:
        copy.wait()


def per_device(fields, spectra, inv_eps, step_phase):
    ns, na = lax.axis_size("slab"), lax.axis_size("angle")
    cols = N // ns
    shape = fields.shape
    vmem = pl.BlockSpec(memory_space=pltpu.VMEM)
    hbm = pl.BlockSpec(memory_space=pltpu.HBM)
    outs = (shape, shape, (2 * NP, cols, N))
    dma = pltpu.SemaphoreType.DMA
    planes = pltpu.VMEM((2, 2, N, N), F32)
    results = pl.pallas_call(
        functools.partial(kernel, ns, na),
        out_shape=[pltpu.VMEM(s, F32) for s in outs],
        in_specs=[hbm, hbm, hbm, pl.BlockSpec(memory_space=pltpu.SMEM)],
        out_specs=[vmem] * 3,
        scratch_shapes=[
            pltpu.VMEM((2, 3, NP + 1, PAD, N), F32),
            pltpu.VMEM((2, 3, NP + 1, PAD, N), F32),
            pltpu.VMEM((NP, N, N), F32),
            pltpu.VMEM((2, 2, PAD, N), F32),
            pltpu.VMEM((2, 2, PAD, N), F32),
            pltpu.VMEM((PAD, N), F32),
            planes, planes, planes, planes, planes, planes,
            pltpu.VMEM((N, N), F32),
            pltpu.VMEM((N, N), F32),
            pltpu.VMEM((NP, N, N), F32),
            pltpu.VMEM((N, N), jnp.bfloat16),
            pltpu.VMEM((N, N), jnp.bfloat16),
            pltpu.VMEM((2, HALF, N, N), F32),
            pltpu.VMEM((2, NP, cols, N), F32),
            pltpu.VMEM((2, na, NP, cols, N), F32),
            planes,
            dma((5,)), dma, dma((3,)), dma, dma((3,)), dma, dma((4,)), dma, dma((2,)), dma, dma((2,)),
        ],
        compiler_params=pltpu.CompilerParams(
            collective_id=0, has_side_effects=True, vmem_limit_bytes=48 * 2**20),
        name="steps",
    )(fields, spectra, inv_eps, step_phase)
    return tuple(pl.pallas_call(
        write_out,
        out_shape=[jax.ShapeDtypeStruct(s, F32) for s in outs],
        in_specs=[vmem] * 3,
        out_specs=[pl.BlockSpec(memory_space=pl.ANY)] * 3,
        scratch_shapes=[dma((3,))],
        compiler_params=pltpu.CompilerParams(has_side_effects=True, vmem_limit_bytes=2**20),
        name="write_out",
    )(*(pltpu.with_memory_space_constraint(r, pltpu.VMEM) for r in results)))


def solution(mesh):
    cells = P("angle", None, None, None, "slab", None, None)
    return jax.shard_map(
        per_device,
        mesh=mesh,
        in_specs=(cells, cells, P("slab", None, None), P()),
        out_specs=(cells, cells, P(None, "slab", None)),
        check_vma=False,
    )
```

```python
import functools

import jax
import jax.numpy as jnp
from jax import lax
from jax.experimental import pallas as pl
from jax.experimental.pallas import tpu as pltpu
from jax.sharding import PartitionSpec as P

MESH = pl.DeviceIdType.MESH
F32 = jnp.float32
N = 128
NP = 4
HALF = NP // 2
PAD = 136
TAPS = (0.375, 0.25, 0.0625)
RELAYED = ((0, 0), (0, 1), (1, 1))
E_ROWS, E_AHEAD = pl.ds(0, N), pl.ds(1, N)
H_ROWS, H_BEHIND = pl.ds(8, N), pl.ds(7, N)


def lane_index(rows):
    return lax.broadcasted_iota(jnp.int32, (rows, N), 1)


def next_y(v):
    return jnp.where(lane_index(v.shape[0]) < N - 1, pltpu.roll(v, N - 1, 1), 0.0)


def prev_y(v):
    return jnp.where(lane_index(v.shape[0]) > 0, pltpu.roll(v, 1, 1), 0.0)


def filter_matrix(mirror):
    row = lax.broadcasted_iota(jnp.int32, (N, N), 0)
    col = lax.broadcasted_iota(jnp.int32, (N, N), 1)

    def taps(distance):
        out = jnp.zeros((N, N), F32)
        for k, tap in enumerate(TAPS):
            out = jnp.where(jnp.abs(distance) == k, tap, out)
        return out

    out = taps(row - col)
    if mirror:
        out = out + taps(row - (N - 1 - col))
    return out


def three_parts(v):
    high = v.astype(jnp.bfloat16)
    rest = v - high.astype(F32)
    mid = rest.astype(jnp.bfloat16)
    low = (rest - mid.astype(F32)).astype(jnp.bfloat16)
    return high, mid, low


def kernel(ns, na, f, sp, ie, ph, fo, so, g, E, H, k, e0h, keep, dz, p1s, p2s, qs, p1r, p2r, qr,
           epsu, epsl, dens, fy, mx, gbuf, r1, r2, rb, in_sem, dn_s, dn_r, up_s, up_r, rl_s, rl_r,
           g1_s, g1_r, g2_s, g2_r, ready):
    slab = lax.axis_index("slab")
    ang = lax.axis_index("angle")
    cols = N // ns
    lo_design, hi_design = ns // 2 - 1, ns // 2
    has_below, has_above = slab > 0, slab < ns - 1
    is_design = jnp.logical_or(slab == lo_design, slab == hi_design)
    relay_up, relay_down = 1, ns - 1
    bar = pltpu.get_barrier_semaphore()

    def signal(slab_index, angle_index):
        pl.semaphore_signal(bar, inc=1, device_id=(slab_index, angle_index), device_id_type=MESH)

    def send(src, dst, send_sem, recv_sem, slab_index, angle_index):
        return pltpu.make_async_remote_copy(
            src_ref=src, dst_ref=dst, send_sem=send_sem, recv_sem=recv_sem,
            device_id=(slab_index, angle_index), device_id_type=MESH)

    def wait_bytes(ref, sem):
        pltpu.make_async_copy(ref, ref, sem).wait()

    pl.when(has_below)(lambda: signal(slab - 1, ang))
    pl.when(has_above)(lambda: signal(slab + 1, ang))
    pl.when(slab == relay_up)(lambda: signal(lo_design, ang))
    pl.when(slab == relay_down)(lambda: signal(hi_design, ang))

    @pl.when(is_design)
    def _():
        for d in range(ns):
            if d not in (lo_design, hi_design):
                signal(d, ang)
        for j in range(1, na):
            signal(jnp.where(slab == lo_design, lo_design - 1, hi_design + 1), lax.rem(ang + j, na))

    @pl.when(jnp.logical_not(is_design))
    def _():
        for j in range(1, na):
            signal(slab, lax.rem(ang + j, na))

    load_keep = pltpu.make_async_copy(f.at[0, :, 0, 0:2, 0], keep.at[:, :, H_ROWS], in_sem.at[3])
    load_keep.start()
    for s in range(2):
        pltpu.make_async_copy(f.at[0, s, 0], E.at[s, :, 0:NP, E_ROWS], in_sem.at[s]).start()
        pltpu.make_async_copy(f.at[0, s, 1], H.at[s, :, 1 : NP + 1, H_ROWS], in_sem.at[s]).start()
        if s == 0:
            load_eps = pltpu.make_async_copy(ie, k, in_sem.at[2])
            load_eps.start()
    load_spectra = pltpu.make_async_copy(sp, so, in_sem.at[4])
    load_spectra.start()

    for s in range(2):
        for c in range(3):
            for z in range(NP):
                E[s, c, z, N:PAD] = jnp.zeros((PAD - N, N), F32)
                H[s, c, z + 1, 0:8] = jnp.zeros((8, N), F32)
        for c in range(2):
            e0h[s, c, 0:8] = jnp.zeros((8, N), F32)
            keep[s, c, 0:8] = jnp.zeros((8, N), F32)
    dz[N:PAD] = jnp.zeros((PAD - N, N), F32)

    @pl.when(slab == 0)
    def _():
        p1r[...] = jnp.zeros_like(p1r)
        p2r[...] = jnp.zeros_like(p2r)
        epsl[...] = jnp.zeros_like(epsl)

    @pl.when(slab == ns - 1)
    def _():
        e0h[...] = jnp.zeros_like(e0h)
        qr[...] = jnp.zeros_like(qr)
        epsu[...] = jnp.zeros_like(epsu)

    def down(src, dst, i):
        return send(src, dst, dn_s, dn_r.at[i], slab - 1, ang)

    def up(src, dst, i):
        return send(src, dst, up_s, up_r.at[i], slab + 1, ang)

    def send_outer(s, src, dst, neighbour, far, relay, exists, send_sem, recv_sem):
        pl.when(jnp.logical_and(exists, slab != far))(
            lambda: send(src.at[s], dst.at[s], send_sem, recv_sem.at[s], neighbour, ang).start())

        @pl.when(slab == far)
        def _():
            for c in range(2):
                if (s, c) in RELAYED:
                    send(src.at[s, c], rb.at[RELAYED.index((s, c))], send_sem, rl_r.at[RELAYED.index((s, c))], relay, ang).start()
            for c in range(2):
                if (s, c) not in RELAYED:
                    send(src.at[s, c], dst.at[s, c], send_sem, recv_sem.at[s], neighbour, ang).start()

    def send_q(s):
        send_outer(s, qs, qr, slab - 1, hi_design, relay_down, has_below, dn_s, dn_r)

    def send_p2(s):
        send_outer(s, p2s, p2r, slab + 1, lo_design, relay_up, has_above, up_s, up_r)

    def pass_on():
        for relay, dst, sems, d in ((relay_up, p2r, up_r, hi_design), (relay_down, qr, dn_r, lo_design)):
            @pl.when(slab == relay)
            def _():
                for i, (s, c) in enumerate(RELAYED):
                    wait_bytes(rb.at[i], rl_r.at[i])
                    send(rb.at[i], dst.at[s, c], rl_s, sems.at[s], d, ang).start()

    def h_new(s, z, top):
        ex, ey, ez = (E[s, c, z, E_ROWS] for c in range(3))
        if top:
            dzx, dzy = -ex, -ey
        else:
            dzx, dzy = E[s, 0, z + 1, E_ROWS] - ex, E[s, 1, z + 1, E_ROWS] - ey
        hx, hy, hz = (H[s, c, z + 1, H_ROWS] for c in range(3))
        hx = hx - 0.5 * ((next_y(ez) - ez) - dzy)
        hy = hy - 0.5 * (dzx - (E[s, 2, z, E_AHEAD] - ez))
        hz = hz - 0.5 * ((E[s, 1, z, E_AHEAD] - ey) - (next_y(ex) - ex))
        return hx, hy, hz

    def e_new(s, z, bottom):
        hx, hy, hz = (H[s, c, z + 1, H_ROWS] for c in range(3))
        if bottom:
            dzx, dzy = hx, hy
        else:
            dzx, dzy = hx - H[s, 0, z, H_ROWS], hy - H[s, 1, z, H_ROWS]
        kk = 0.5 * k[z]
        old = tuple(E[s, c, z, E_ROWS] for c in range(3))
        ex = old[0] + kk * ((hz - prev_y(hz)) - dzy)
        ey = old[1] + kk * (dzx - (hz - H[s, 2, z + 1, H_BEHIND]))
        ez = old[2] + kk * ((hy - H[s, 1, z + 1, H_BEHIND]) - (hx - prev_y(hx)))
        return old, (ex, ey, ez)

    def first_step(s):
        for z in range(NP):
            new = h_new(s, z, z == NP - 1)
            for c in range(3):
                H[s, c, z + 1, H_ROWS] = new[c]
        for c in range(2):
            p1s[s, c] = new[c]
        for z in range(NP):
            _, new = e_new(s, z, z == 0)
            for c in range(3):
                E[s, c, z, E_ROWS] = new[c]
                if z == 0 and c < 2:
                    qs[s, c] = new[c]
        new = h_new(s, NP - 1, True)
        for c in range(2):
            p2s[s, c] = new[c]

    edge = jnp.where(has_below, 0.5, 0.0).astype(F32)

    def fix_above(s):
        dx, dy = 0.5 * e0h[s, 1, H_ROWS], -0.5 * e0h[s, 0, H_ROWS]
        hx, hy = H[s, 0, NP, H_ROWS] + dx, H[s, 1, NP, H_ROWS] + dy
        H[s, 0, NP, H_ROWS] = hx
        H[s, 1, NP, H_ROWS] = hy
        k3 = 0.5 * k[NP - 1]
        E[s, 0, NP - 1, E_ROWS] = E[s, 0, NP - 1, E_ROWS] - k3 * dy
        E[s, 1, NP - 1, E_ROWS] = E[s, 1, NP - 1, E_ROWS] + k3 * dx
        E[s, 2, NP - 1, E_ROWS] = E[s, 2, NP - 1, E_ROWS] + k3 * (
            (dy + 0.5 * e0h[s, 0, H_BEHIND]) - (dx - prev_y(dx)))
        ku = 0.5 * epsu[...]
        E[s, 0, NP, E_ROWS] = qr[s, 0] + ku * hy
        E[s, 1, NP, E_ROWS] = qr[s, 1] - ku * hx

    def fix_below(s):
        dx, dy = edge * keep[s, 1, H_ROWS], -edge * keep[s, 0, H_ROWS]
        k0, kl = 0.5 * k[0], 0.5 * epsl[...]
        d = kl * ((dy + edge * keep[s, 0, H_BEHIND]) - (dx - prev_y(dx)))
        dz[E_ROWS] = d
        ex = E[s, 0, 0, E_ROWS] + k0 * (p1r[s, 1] + dy)
        ey = E[s, 1, 0, E_ROWS] - k0 * (p1r[s, 0] + dx)
        E[s, 0, 0, E_ROWS] = ex
        E[s, 1, 0, E_ROWS] = ey
        H[s, 0, 0, H_ROWS] = p2r[s, 0] + dx - 0.5 * (next_y(d) - d) + (edge * ey - 0.5 * kl * dx)
        H[s, 1, 0, H_ROWS] = p2r[s, 1] + dy + 0.5 * (dz[E_AHEAD] - d) - (edge * ex + 0.5 * kl * dy)

    def second_h(s, planes):
        for z in planes:
            new = h_new(s, z, False)
            for c in range(3):
                H[s, c, z + 1, H_ROWS] = new[c]
                fo[0, s, 1, c, z] = new[c]

    def second_e(s, planes):
        c0, s0, c1, s1 = (op(jnp.full((1, N), ph[t], F32)) for t in range(2) for op in (jnp.cos, jnp.sin))
        for z in planes:
            old, new = e_new(s, z, False)
            total = jnp.zeros((N, N), F32)
            for c in range(3):
                fo[0, s, 0, c, z] = new[c]
                re = so[0, s, 0, c, z] + old[c] * c0 + new[c] * c1
                im = so[0, s, 1, c, z] + old[c] * s0 + new[c] * s1
                so[0, s, 0, c, z] = re
                so[0, s, 1, c, z] = im
                if s == 1:
                    total = total + so[0, 0, 0, c, z] * re - so[0, 0, 1, c, z] * im
            if s == 1:
                dens[z] = total

    def lower_planes(s):
        @pl.when(has_below)
        def _():
            if s == 0:
                wait_bytes(epsl, up_r.at[2])
            wait_bytes(fo.at[0, s, 0, 0], up_r.at[s])

        fix_below(s)
        second_h(s, (0,))
        second_e(s, (0, 1))

    def upper_planes(s):
        @pl.when(has_above)
        def _():
            if s == 0:
                wait_bytes(epsu, dn_r.at[2])
            wait_bytes(fo.at[0, s, 0, 0], dn_r.at[s])

        fix_above(s)
        second_h(s, (2, 3))
        second_e(s, (2, 3))

    wait_bytes(so.at[0, 0], in_sem.at[0])
    load_eps.wait()
    load_keep.wait()
    first_step(0)
    incoming = jnp.where(has_below, 1, 0) + jnp.where(has_above, 1, 0)
    incoming = incoming + jnp.where(is_design, 1, 2 + na - 1)
    incoming = incoming + jnp.where(jnp.logical_or(slab == lo_design - 1, slab == hi_design + 1), na - 1, 0)
    pl.semaphore_wait(bar, incoming)

    @pl.when(jnp.logical_not(is_design))
    def _():
        for d in (lo_design, hi_design):
            pl.semaphore_signal(ready, inc=1, device_id=(d, ang), device_id_type=MESH)

    @pl.when(has_below)
    def _():
        down(k.at[0], epsu, 2).start()
        for s in range(2):
            down(keep.at[s, :, H_ROWS], e0h.at[s, :, H_ROWS], s).start()

    @pl.when(has_above)
    def _():
        up(k.at[NP - 1], epsl, 2).start()
        up(p1s.at[0], p1r.at[0], 0).start()

    send_q(0)
    send_p2(0)
    wait_bytes(so.at[0, 1], in_sem.at[1])
    first_step(1)
    pl.when(has_above)(lambda: up(p1s.at[1], p1r.at[1], 1).start())
    send_q(1)
    send_p2(1)
    pass_on()
    for s in range(2):
        second_h(s, (1,))
    fy[...] = filter_matrix(False).astype(jnp.bfloat16)
    mx[...] = (filter_matrix(True) * (0.5 / na)).astype(jnp.bfloat16)
    load_spectra.wait()

    def to_owner(part, side, owner):
        return send(gbuf.at[part, :, pl.ds(owner * cols, cols)], r1.at[part, pl.ds(side * HALF, HALF)],
                    g1_s, g1_r.at[part], owner, ang)

    def spread_density(part, first, side):
        planes = dens[first : first + HALF].reshape(HALF * N, N)
        along_y = sum(jnp.dot(p, fy[...], preferred_element_type=F32) for p in three_parts(planes))
        beside = jnp.concatenate([along_y[z * N : (z + 1) * N] for z in range(HALF)], axis=1)
        both = sum(jnp.dot(mx[...], p, preferred_element_type=F32) for p in three_parts(beside))
        for z in range(HALF):
            gbuf[part, z] = both[:, z * N : (z + 1) * N]
        d = (lo_design, hi_design)[side]
        for owner in range(ns):
            if owner != d:
                to_owner(part, side, owner).start()
        r1[part, side * HALF : (side + 1) * HALF] = gbuf[part, :, d * cols : (d + 1) * cols]

    def beside_core(planes_below):
        for odd, planes in ((1, lower_planes), (0, upper_planes)):
            @pl.when(slab % 2 == (odd if planes_below else 1 - odd))
            def _():
                for s in range(2):
                    planes(s)

    beside_core(True)
    pl.when(is_design)(lambda: pl.semaphore_wait(ready, ns - 2))
    for side, d in enumerate((lo_design, hi_design)):
        pl.when(slab == d)(functools.partial(spread_density, 0, HALF * side, side))

    @pl.when(slab == lo_design)
    def _():
        for s in range(2):
            upper_planes(s)
        spread_density(1, HALF, 0)

    @pl.when(slab == hi_design)
    def _():
        for s in range(2):
            lower_planes(s)
        spread_density(1, 0, 1)

    for part in (0, 1):
        pl.when(is_design)(lambda: wait_bytes(r1.at[part, pl.ds(0, HALF)], g1_r.at[part]))
        pl.when(jnp.logical_not(is_design))(lambda: wait_bytes(r1.at[part], g1_r.at[part]))
        for j in range(1, na):
            send(r1.at[part], r2.at[part, ang], g2_s, g2_r.at[part], slab, lax.rem(ang + j, na)).start()
        r2[part, ang] = r1[part]

    pl.when(jnp.logical_not(is_design))(lambda: beside_core(False))

    for part in (0, 1):
        wait_bytes(r2.at[part, pl.ds(0, na - 1)], g2_r.at[part])
        total = r2[part, 0]
        for j in range(1, na):
            total = total + r2[part, j]
        if part == 0:
            g[0:HALF] = total[0:HALF]
            g[NP + HALF :] = total[HALF:]
        else:
            g[HALF : NP + HALF] = total

    wait_bytes(r2.at[:, pl.ds(0, na - 1)], g2_s)
    nine_planes = E.at[0, 0:3, 0:3, E_ROWS]
    pl.when(has_below)(lambda: wait_bytes(nine_planes, dn_s))
    pl.when(has_above)(lambda: wait_bytes(nine_planes, up_s))
    pl.when(jnp.logical_or(slab == relay_up, slab == relay_down))(lambda: wait_bytes(rb, rl_s))
    pl.when(is_design)(lambda: wait_bytes(gbuf.at[:, :, pl.ds(0, N - cols)], g1_s))


def write_out(a, b, c, x, y, z, sem):
    copies = [pltpu.make_async_copy(p, q, sem.at[i]) for i, (p, q) in enumerate(((a, x), (b, y), (c, z)))]
    for copy in copies:
        copy.start()
    for copy in copies:
        copy.wait()


def per_device(fields, spectra, inv_eps, step_phase):
    ns, na = lax.axis_size("slab"), lax.axis_size("angle")
    cols = N // ns
    shape = fields.shape
    vmem = pl.BlockSpec(memory_space=pltpu.VMEM)
    hbm = pl.BlockSpec(memory_space=pltpu.HBM)
    outs = (shape, shape, (2 * NP, cols, N))
    dma = pltpu.SemaphoreType.DMA
    planes = pltpu.VMEM((2, 2, N, N), F32)
    results = pl.pallas_call(
        functools.partial(kernel, ns, na),
        out_shape=[pltpu.VMEM(s, F32) for s in outs],
        in_specs=[hbm, hbm, hbm, pl.BlockSpec(memory_space=pltpu.SMEM)],
        out_specs=[vmem] * 3,
        scratch_shapes=[
            pltpu.VMEM((2, 3, NP + 1, PAD, N), F32),
            pltpu.VMEM((2, 3, NP + 1, PAD, N), F32),
            pltpu.VMEM((NP, N, N), F32),
            pltpu.VMEM((2, 2, PAD, N), F32),
            pltpu.VMEM((2, 2, PAD, N), F32),
            pltpu.VMEM((PAD, N), F32),
            planes, planes, planes, planes, planes, planes,
            pltpu.VMEM((N, N), F32),
            pltpu.VMEM((N, N), F32),
            pltpu.VMEM((NP, N, N), F32),
            pltpu.VMEM((N, N), jnp.bfloat16),
            pltpu.VMEM((N, N), jnp.bfloat16),
            pltpu.VMEM((2, HALF, N, N), F32),
            pltpu.VMEM((2, NP, cols, N), F32),
            pltpu.VMEM((2, na, NP, cols, N), F32),
            pltpu.VMEM((len(RELAYED), N, N), F32),
            dma((5,)), dma, dma((3,)), dma, dma((3,)), dma, dma((len(RELAYED),)), dma, dma((2,)), dma, dma((2,)),
            pltpu.SemaphoreType.REGULAR,
        ],
        compiler_params=pltpu.CompilerParams(
            collective_id=0, has_side_effects=True, vmem_limit_bytes=48 * 2**20),
        name="steps",
    )(fields, spectra, inv_eps, step_phase)
    return tuple(pl.pallas_call(
        write_out,
        out_shape=[jax.ShapeDtypeStruct(s, F32) for s in outs],
        in_specs=[vmem] * 3,
        out_specs=[pl.BlockSpec(memory_space=pl.ANY)] * 3,
        scratch_shapes=[dma((3,))],
        compiler_params=pltpu.CompilerParams(has_side_effects=True, vmem_limit_bytes=2**20),
        name="write_out",
    )(*(pltpu.with_memory_space_constraint(r, pltpu.VMEM) for r in results)))


def solution(mesh):
    cells = P("angle", None, None, None, "slab", None, None)
    return jax.shard_map(
        per_device,
        mesh=mesh,
        in_specs=(cells, cells, P("slab", None, None), P()),
        out_specs=(cells, cells, P(None, "slab", None)),
        check_vma=False,
    )
```

```python
import functools

import jax
import jax.numpy as jnp
from jax import lax
from jax.experimental import pallas as pl
from jax.experimental.pallas import tpu as pltpu
from jax.sharding import PartitionSpec as P

MESH = pl.DeviceIdType.MESH
F32 = jnp.float32
N = 128
NP = 4
HALF = NP // 2
PAD = 136
TAPS = (0.375, 0.25, 0.0625)
RELAYED = ((0, 0), (0, 1), (1, 1))
E_ROWS, E_AHEAD = pl.ds(0, N), pl.ds(1, N)
H_ROWS, H_BEHIND = pl.ds(8, N), pl.ds(7, N)


def lane_index(rows):
    return lax.broadcasted_iota(jnp.int32, (rows, N), 1)


def next_y(v):
    return jnp.where(lane_index(v.shape[0]) < N - 1, pltpu.roll(v, N - 1, 1), 0.0)


def prev_y(v):
    return jnp.where(lane_index(v.shape[0]) > 0, pltpu.roll(v, 1, 1), 0.0)


def filter_matrix(mirror):
    row = lax.broadcasted_iota(jnp.int32, (N, N), 0)
    col = lax.broadcasted_iota(jnp.int32, (N, N), 1)

    def taps(distance):
        out = jnp.zeros((N, N), F32)
        for k, tap in enumerate(TAPS):
            out = jnp.where(jnp.abs(distance) == k, tap, out)
        return out

    out = taps(row - col)
    if mirror:
        out = out + taps(row - (N - 1 - col))
    return out


def three_parts(v):
    high = v.astype(jnp.bfloat16)
    rest = v - high.astype(F32)
    mid = rest.astype(jnp.bfloat16)
    low = (rest - mid.astype(F32)).astype(jnp.bfloat16)
    return high, mid, low


def kernel(ns, na, f, sp, ie, ph, fo, so, g, E, H, k, e0h, keep, dz, p1s, p2s, qs, p1r, p2r, qr,
           epsu, epsl, dens, fy, mx, gbuf, r1, r2, rb, in_sem, dn_s, dn_r, up_s, up_r, rl_s, rl_r,
           g1_s, g1_r, g2_s, g2_r, ready):
    slab = lax.axis_index("slab")
    ang = lax.axis_index("angle")
    cols = N // ns
    lo_design, hi_design = ns // 2 - 1, ns // 2
    has_below, has_above = slab > 0, slab < ns - 1
    is_design = jnp.logical_or(slab == lo_design, slab == hi_design)
    relay_up, relay_down = 1, ns - 1
    bar = pltpu.get_barrier_semaphore()

    def signal(slab_index, angle_index):
        pl.semaphore_signal(bar, inc=1, device_id=(slab_index, angle_index), device_id_type=MESH)

    def send(src, dst, send_sem, recv_sem, slab_index, angle_index):
        return pltpu.make_async_remote_copy(
            src_ref=src, dst_ref=dst, send_sem=send_sem, recv_sem=recv_sem,
            device_id=(slab_index, angle_index), device_id_type=MESH)

    def wait_bytes(ref, sem):
        pltpu.make_async_copy(ref, ref, sem).wait()

    pl.when(has_below)(lambda: signal(slab - 1, ang))
    pl.when(has_above)(lambda: signal(slab + 1, ang))
    pl.when(slab == relay_up)(lambda: signal(lo_design, ang))
    pl.when(slab == relay_down)(lambda: signal(hi_design, ang))

    @pl.when(is_design)
    def _():
        for d in range(ns):
            if d not in (lo_design, hi_design):
                signal(d, ang)
        for j in range(1, na):
            signal(jnp.where(slab == lo_design, lo_design - 1, hi_design + 1), lax.rem(ang + j, na))

    @pl.when(jnp.logical_not(is_design))
    def _():
        for j in range(1, na):
            signal(slab, lax.rem(ang + j, na))

    load_keep = pltpu.make_async_copy(f.at[0, :, 0, 0:2, 0], keep.at[:, :, H_ROWS], in_sem.at[3])
    load_keep.start()
    for s in range(2):
        pltpu.make_async_copy(f.at[0, s, 0], E.at[s, :, 0:NP, E_ROWS], in_sem.at[s]).start()
        pltpu.make_async_copy(f.at[0, s, 1], H.at[s, :, 1 : NP + 1, H_ROWS], in_sem.at[s]).start()
        if s == 0:
            load_eps = pltpu.make_async_copy(ie, k, in_sem.at[2])
            load_eps.start()
    load_spectra = pltpu.make_async_copy(sp, so, in_sem.at[4])
    load_spectra.start()

    for s in range(2):
        for c in range(3):
            for z in range(NP):
                E[s, c, z, N:PAD] = jnp.zeros((PAD - N, N), F32)
                H[s, c, z + 1, 0:8] = jnp.zeros((8, N), F32)
        for c in range(2):
            e0h[s, c, 0:8] = jnp.zeros((8, N), F32)
            keep[s, c, 0:8] = jnp.zeros((8, N), F32)
    dz[N:PAD] = jnp.zeros((PAD - N, N), F32)

    @pl.when(slab == 0)
    def _():
        p1r[...] = jnp.zeros_like(p1r)
        p2r[...] = jnp.zeros_like(p2r)
        epsl[...] = jnp.zeros_like(epsl)

    @pl.when(slab == ns - 1)
    def _():
        e0h[...] = jnp.zeros_like(e0h)
        qr[...] = jnp.zeros_like(qr)
        epsu[...] = jnp.zeros_like(epsu)

    def down(src, dst, i):
        return send(src, dst, dn_s, dn_r.at[i], slab - 1, ang)

    def up(src, dst, i):
        return send(src, dst, up_s, up_r.at[i], slab + 1, ang)

    def send_outer(s, src, dst, neighbour, far, relay, exists, send_sem, recv_sem):
        pl.when(jnp.logical_and(exists, slab != far))(
            lambda: send(src.at[s], dst.at[s], send_sem, recv_sem.at[s], neighbour, ang).start())

        @pl.when(slab == far)
        def _():
            for c in range(2):
                if (s, c) in RELAYED:
                    send(src.at[s, c], rb.at[RELAYED.index((s, c))], send_sem, rl_r.at[RELAYED.index((s, c))], relay, ang).start()
            for c in range(2):
                if (s, c) not in RELAYED:
                    send(src.at[s, c], dst.at[s, c], send_sem, recv_sem.at[s], neighbour, ang).start()

    def send_q(s):
        send_outer(s, qs, qr, slab - 1, hi_design, relay_down, has_below, dn_s, dn_r)

    def send_p2(s):
        send_outer(s, p2s, p2r, slab + 1, lo_design, relay_up, has_above, up_s, up_r)

    def pass_on():
        for relay, dst, sems, d in ((relay_up, p2r, up_r, hi_design), (relay_down, qr, dn_r, lo_design)):
            @pl.when(slab == relay)
            def _():
                for i, (s, c) in enumerate(RELAYED):
                    wait_bytes(rb.at[i], rl_r.at[i])
                    send(rb.at[i], dst.at[s, c], rl_s, sems.at[s], d, ang).start()

    def h_new(s, z, top):
        ex, ey, ez = (E[s, c, z, E_ROWS] for c in range(3))
        if top:
            dzx, dzy = -ex, -ey
        else:
            dzx, dzy = E[s, 0, z + 1, E_ROWS] - ex, E[s, 1, z + 1, E_ROWS] - ey
        hx, hy, hz = (H[s, c, z + 1, H_ROWS] for c in range(3))
        hx = hx - 0.5 * ((next_y(ez) - ez) - dzy)
        hy = hy - 0.5 * (dzx - (E[s, 2, z, E_AHEAD] - ez))
        hz = hz - 0.5 * ((E[s, 1, z, E_AHEAD] - ey) - (next_y(ex) - ex))
        return hx, hy, hz

    def e_new(s, z, bottom):
        hx, hy, hz = (H[s, c, z + 1, H_ROWS] for c in range(3))
        if bottom:
            dzx, dzy = hx, hy
        else:
            dzx, dzy = hx - H[s, 0, z, H_ROWS], hy - H[s, 1, z, H_ROWS]
        kk = 0.5 * k[z]
        old = tuple(E[s, c, z, E_ROWS] for c in range(3))
        ex = old[0] + kk * ((hz - prev_y(hz)) - dzy)
        ey = old[1] + kk * (dzx - (hz - H[s, 2, z + 1, H_BEHIND]))
        ez = old[2] + kk * ((hy - H[s, 1, z + 1, H_BEHIND]) - (hx - prev_y(hx)))
        return old, (ex, ey, ez)

    def first_step(s):
        for z in range(NP):
            new = h_new(s, z, z == NP - 1)
            for c in range(3):
                H[s, c, z + 1, H_ROWS] = new[c]
        for c in range(2):
            p1s[s, c] = new[c]
        for z in range(NP):
            _, new = e_new(s, z, z == 0)
            for c in range(3):
                E[s, c, z, E_ROWS] = new[c]
                if z == 0 and c < 2:
                    qs[s, c] = new[c]
        new = h_new(s, NP - 1, True)
        for c in range(2):
            p2s[s, c] = new[c]

    edge = jnp.where(has_below, 0.5, 0.0).astype(F32)

    def fix_above(s):
        dx, dy = 0.5 * e0h[s, 1, H_ROWS], -0.5 * e0h[s, 0, H_ROWS]
        hx, hy = H[s, 0, NP, H_ROWS] + dx, H[s, 1, NP, H_ROWS] + dy
        H[s, 0, NP, H_ROWS] = hx
        H[s, 1, NP, H_ROWS] = hy
        k3 = 0.5 * k[NP - 1]
        E[s, 0, NP - 1, E_ROWS] = E[s, 0, NP - 1, E_ROWS] - k3 * dy
        E[s, 1, NP - 1, E_ROWS] = E[s, 1, NP - 1, E_ROWS] + k3 * dx
        E[s, 2, NP - 1, E_ROWS] = E[s, 2, NP - 1, E_ROWS] + k3 * (
            (dy + 0.5 * e0h[s, 0, H_BEHIND]) - (dx - prev_y(dx)))
        ku = 0.5 * epsu[...]
        E[s, 0, NP, E_ROWS] = qr[s, 0] + ku * hy
        E[s, 1, NP, E_ROWS] = qr[s, 1] - ku * hx

    def fix_below(s):
        dx, dy = edge * keep[s, 1, H_ROWS], -edge * keep[s, 0, H_ROWS]
        k0, kl = 0.5 * k[0], 0.5 * epsl[...]
        d = kl * ((dy + edge * keep[s, 0, H_BEHIND]) - (dx - prev_y(dx)))
        dz[E_ROWS] = d
        ex = E[s, 0, 0, E_ROWS] + k0 * (p1r[s, 1] + dy)
        ey = E[s, 1, 0, E_ROWS] - k0 * (p1r[s, 0] + dx)
        E[s, 0, 0, E_ROWS] = ex
        E[s, 1, 0, E_ROWS] = ey
        H[s, 0, 0, H_ROWS] = p2r[s, 0] + dx - 0.5 * (next_y(d) - d) + (edge * ey - 0.5 * kl * dx)
        H[s, 1, 0, H_ROWS] = p2r[s, 1] + dy + 0.5 * (dz[E_AHEAD] - d) - (edge * ex + 0.5 * kl * dy)

    def second_h(s, planes):
        for z in planes:
            new = h_new(s, z, False)
            for c in range(3):
                H[s, c, z + 1, H_ROWS] = new[c]
                fo[0, s, 1, c, z] = new[c]

    def second_e(s, planes):
        c0, s0, c1, s1 = (op(jnp.full((1, N), ph[t], F32)) for t in range(2) for op in (jnp.cos, jnp.sin))
        for z in planes:
            old, new = e_new(s, z, False)
            total = jnp.zeros((N, N), F32)
            for c in range(3):
                fo[0, s, 0, c, z] = new[c]
                re = so[0, s, 0, c, z] + old[c] * c0 + new[c] * c1
                im = so[0, s, 1, c, z] + old[c] * s0 + new[c] * s1
                so[0, s, 0, c, z] = re
                so[0, s, 1, c, z] = im
                if s == 1:
                    total = total + so[0, 0, 0, c, z] * re - so[0, 0, 1, c, z] * im
            if s == 1:
                dens[z] = total

    def lower_planes(s):
        @pl.when(has_below)
        def _():
            if s == 0:
                wait_bytes(epsl, up_r.at[2])
            wait_bytes(fo.at[0, s, 0, 0], up_r.at[s])

        fix_below(s)
        second_h(s, (0,))
        second_e(s, (0, 1))

    def upper_planes(s):
        @pl.when(has_above)
        def _():
            if s == 0:
                wait_bytes(epsu, dn_r.at[2])
            wait_bytes(fo.at[0, s, 0, 0], dn_r.at[s])

        fix_above(s)
        second_h(s, (2, 3))
        second_e(s, (2, 3))

    wait_bytes(so.at[0, 0], in_sem.at[0])
    load_eps.wait()
    load_keep.wait()
    first_step(0)
    incoming = jnp.where(has_below, 1, 0) + jnp.where(has_above, 1, 0)
    incoming = incoming + jnp.where(is_design, 1, 2 + na - 1)
    incoming = incoming + jnp.where(jnp.logical_or(slab == lo_design - 1, slab == hi_design + 1), na - 1, 0)
    pl.semaphore_wait(bar, incoming)

    @pl.when(jnp.logical_not(is_design))
    def _():
        for d in (lo_design, hi_design):
            pl.semaphore_signal(ready, inc=1, device_id=(d, ang), device_id_type=MESH)

    @pl.when(has_below)
    def _():
        down(k.at[0], epsu, 2).start()
        for s in range(2):
            down(keep.at[s, :, H_ROWS], e0h.at[s, :, H_ROWS], s).start()

    @pl.when(has_above)
    def _():
        up(k.at[NP - 1], epsl, 2).start()
        up(p1s.at[0], p1r.at[0], 0).start()

    send_q(0)
    send_p2(0)
    wait_bytes(so.at[0, 1], in_sem.at[1])
    first_step(1)
    pl.when(has_above)(lambda: up(p1s.at[1], p1r.at[1], 1).start())
    send_q(1)
    send_p2(1)
    pass_on()
    for s in range(2):
        second_h(s, (1,))
    fy[...] = jnp.concatenate([filter_matrix(False).astype(jnp.bfloat16)] * 3, axis=0)
    mx[...] = jnp.concatenate([(filter_matrix(True) * (0.5 / na)).astype(jnp.bfloat16)] * 3, axis=1)
    load_spectra.wait()

    def to_owner(part, side, owner):
        return send(gbuf.at[part, :, pl.ds(owner * cols, cols)], r1.at[part, pl.ds(side * HALF, HALF)],
                    g1_s, g1_r.at[part], owner, ang)

    def spread_density(part, first, side):
        planes = dens[first : first + HALF].reshape(HALF * N, N)
        along_y = jnp.dot(jnp.concatenate(three_parts(planes), axis=1), fy[...], preferred_element_type=F32)
        beside = jnp.concatenate([along_y[z * N : (z + 1) * N] for z in range(HALF)], axis=1)
        both = jnp.dot(mx[...], jnp.concatenate(three_parts(beside), axis=0), preferred_element_type=F32)
        for z in range(HALF):
            gbuf[part, z] = both[:, z * N : (z + 1) * N]
        d = (lo_design, hi_design)[side]
        for owner in range(ns):
            if owner != d:
                to_owner(part, side, owner).start()
        r1[part, side * HALF : (side + 1) * HALF] = gbuf[part, :, d * cols : (d + 1) * cols]

    def beside_core(planes_below):
        for odd, planes in ((1, lower_planes), (0, upper_planes)):
            @pl.when(slab % 2 == (odd if planes_below else 1 - odd))
            def _():
                for s in range(2):
                    planes(s)

    beside_core(True)
    pl.when(is_design)(lambda: pl.semaphore_wait(ready, ns - 2))
    for side, d in enumerate((lo_design, hi_design)):
        pl.when(slab == d)(functools.partial(spread_density, 0, HALF * side, side))

    @pl.when(slab == lo_design)
    def _():
        for s in range(2):
            upper_planes(s)
        spread_density(1, HALF, 0)

    @pl.when(slab == hi_design)
    def _():
        for s in range(2):
            lower_planes(s)
        spread_density(1, 0, 1)

    for part in (0, 1):
        pl.when(is_design)(lambda: wait_bytes(r1.at[part, pl.ds(0, HALF)], g1_r.at[part]))
        pl.when(jnp.logical_not(is_design))(lambda: wait_bytes(r1.at[part], g1_r.at[part]))
        for j in range(1, na):
            send(r1.at[part], r2.at[part, ang], g2_s, g2_r.at[part], slab, lax.rem(ang + j, na)).start()
        r2[part, ang] = r1[part]

    pl.when(jnp.logical_not(is_design))(lambda: beside_core(False))

    for part in (0, 1):
        wait_bytes(r2.at[part, pl.ds(0, na - 1)], g2_r.at[part])
        total = r2[part, 0]
        for j in range(1, na):
            total = total + r2[part, j]
        if part == 0:
            g[0:HALF] = total[0:HALF]
            g[NP + HALF :] = total[HALF:]
        else:
            g[HALF : NP + HALF] = total

    wait_bytes(r2.at[:, pl.ds(0, na - 1)], g2_s)
    nine_planes = E.at[0, 0:3, 0:3, E_ROWS]
    pl.when(has_below)(lambda: wait_bytes(nine_planes, dn_s))
    pl.when(has_above)(lambda: wait_bytes(nine_planes, up_s))
    pl.when(jnp.logical_or(slab == relay_up, slab == relay_down))(lambda: wait_bytes(rb, rl_s))
    pl.when(is_design)(lambda: wait_bytes(gbuf.at[:, :, pl.ds(0, N - cols)], g1_s))


def write_out(a, b, c, x, y, z, sem):
    copies = [pltpu.make_async_copy(p, q, sem.at[i]) for i, (p, q) in enumerate(((a, x), (b, y), (c, z)))]
    for copy in copies:
        copy.start()
    for copy in copies:
        copy.wait()


def per_device(fields, spectra, inv_eps, step_phase):
    ns, na = lax.axis_size("slab"), lax.axis_size("angle")
    cols = N // ns
    shape = fields.shape
    vmem = pl.BlockSpec(memory_space=pltpu.VMEM)
    hbm = pl.BlockSpec(memory_space=pltpu.HBM)
    outs = (shape, shape, (2 * NP, cols, N))
    dma = pltpu.SemaphoreType.DMA
    planes = pltpu.VMEM((2, 2, N, N), F32)
    results = pl.pallas_call(
        functools.partial(kernel, ns, na),
        out_shape=[pltpu.VMEM(s, F32) for s in outs],
        in_specs=[hbm, hbm, hbm, pl.BlockSpec(memory_space=pltpu.SMEM)],
        out_specs=[vmem] * 3,
        scratch_shapes=[
            pltpu.VMEM((2, 3, NP + 1, PAD, N), F32),
            pltpu.VMEM((2, 3, NP + 1, PAD, N), F32),
            pltpu.VMEM((NP, N, N), F32),
            pltpu.VMEM((2, 2, PAD, N), F32),
            pltpu.VMEM((2, 2, PAD, N), F32),
            pltpu.VMEM((PAD, N), F32),
            planes, planes, planes, planes, planes, planes,
            pltpu.VMEM((N, N), F32),
            pltpu.VMEM((N, N), F32),
            pltpu.VMEM((NP, N, N), F32),
            pltpu.VMEM((3 * N, N), jnp.bfloat16),
            pltpu.VMEM((N, 3 * N), jnp.bfloat16),
            pltpu.VMEM((2, HALF, N, N), F32),
            pltpu.VMEM((2, NP, cols, N), F32),
            pltpu.VMEM((2, na, NP, cols, N), F32),
            pltpu.VMEM((len(RELAYED), N, N), F32),
            dma((5,)), dma, dma((3,)), dma, dma((3,)), dma, dma((len(RELAYED),)), dma, dma((2,)), dma, dma((2,)),
            pltpu.SemaphoreType.REGULAR,
        ],
        compiler_params=pltpu.CompilerParams(
            collective_id=0, has_side_effects=True, vmem_limit_bytes=48 * 2**20),
        name="steps",
    )(fields, spectra, inv_eps, step_phase)
    return tuple(pl.pallas_call(
        write_out,
        out_shape=[jax.ShapeDtypeStruct(s, F32) for s in outs],
        in_specs=[vmem] * 3,
        out_specs=[pl.BlockSpec(memory_space=pl.ANY)] * 3,
        scratch_shapes=[dma((3,))],
        compiler_params=pltpu.CompilerParams(has_side_effects=True, vmem_limit_bytes=2**20),
        name="write_out",
    )(*(pltpu.with_memory_space_constraint(r, pltpu.VMEM) for r in results)))


def solution(mesh):
    cells = P("angle", None, None, None, "slab", None, None)
    return jax.shard_map(
        per_device,
        mesh=mesh,
        in_specs=(cells, cells, P("slab", None, None), P()),
        out_specs=(cells, cells, P(None, "slab", None)),
        check_vma=False,
    )
```

```python
import functools

import jax
import jax.numpy as jnp
from jax import lax
from jax.experimental import pallas as pl
from jax.experimental.pallas import tpu as pltpu
from jax.sharding import PartitionSpec as P

MESH = pl.DeviceIdType.MESH
F32 = jnp.float32
N = 128
NP = 4
HALF = NP // 2
PAD = 136
TAPS = (0.375, 0.25, 0.0625)
RELAYED = ((0, 0), (0, 1), (1, 1))
E_ROWS, E_AHEAD = pl.ds(0, N), pl.ds(1, N)
H_ROWS, H_BEHIND = pl.ds(8, N), pl.ds(7, N)


def lane_index(rows):
    return lax.broadcasted_iota(jnp.int32, (rows, N), 1)


def next_y(v):
    return jnp.where(lane_index(v.shape[0]) < N - 1, pltpu.roll(v, N - 1, 1), 0.0)


def prev_y(v):
    return jnp.where(lane_index(v.shape[0]) > 0, pltpu.roll(v, 1, 1), 0.0)


def filter_matrix(mirror):
    row = lax.broadcasted_iota(jnp.int32, (N, N), 0)
    col = lax.broadcasted_iota(jnp.int32, (N, N), 1)

    def taps(distance):
        out = jnp.zeros((N, N), F32)
        for k, tap in enumerate(TAPS):
            out = jnp.where(jnp.abs(distance) == k, tap, out)
        return out

    out = taps(row - col)
    if mirror:
        out = out + taps(row - (N - 1 - col))
    return out


def three_parts(v):
    high = v.astype(jnp.bfloat16)
    rest = v - high.astype(F32)
    mid = rest.astype(jnp.bfloat16)
    low = (rest - mid.astype(F32)).astype(jnp.bfloat16)
    return high, mid, low


def kernel(ns, na, f, sp, ie, ph, fo, so, g, E, H, k, e0h, keep, dz, p1s, p2s, qs, p1r, p2r, qr,
           epsu, epsl, dens, fy, mx, gbuf, r1, r2, rb, in_sem, dn_s, dn_r, up_s, up_r, rl_s, rl_r,
           g1_s, g1_r, g2_s, g2_r, ready):
    slab = lax.axis_index("slab")
    ang = lax.axis_index("angle")
    cols = N // ns
    lo_design, hi_design = ns // 2 - 1, ns // 2
    has_below, has_above = slab > 0, slab < ns - 1
    is_design = jnp.logical_or(slab == lo_design, slab == hi_design)
    relay_up, relay_down = 1, ns - 1
    bar = pltpu.get_barrier_semaphore()

    def signal(slab_index, angle_index):
        pl.semaphore_signal(bar, inc=1, device_id=(slab_index, angle_index), device_id_type=MESH)

    def send(src, dst, send_sem, recv_sem, slab_index, angle_index):
        return pltpu.make_async_remote_copy(
            src_ref=src, dst_ref=dst, send_sem=send_sem, recv_sem=recv_sem,
            device_id=(slab_index, angle_index), device_id_type=MESH)

    def wait_bytes(ref, sem):
        pltpu.make_async_copy(ref, ref, sem).wait()

    pl.when(has_below)(lambda: signal(slab - 1, ang))
    pl.when(has_above)(lambda: signal(slab + 1, ang))
    pl.when(slab == relay_up)(lambda: signal(lo_design, ang))
    pl.when(slab == relay_down)(lambda: signal(hi_design, ang))

    @pl.when(is_design)
    def _():
        for d in range(ns):
            if d not in (lo_design, hi_design):
                signal(d, ang)
        for j in range(1, na):
            signal(jnp.where(slab == lo_design, lo_design - 1, hi_design + 1), lax.rem(ang + j, na))

    @pl.when(jnp.logical_not(is_design))
    def _():
        for j in range(1, na):
            signal(slab, lax.rem(ang + j, na))

    load_keep = pltpu.make_async_copy(f.at[0, :, 0, 0:2, 0], keep.at[:, :, H_ROWS], in_sem.at[3])
    load_keep.start()
    for s in range(2):
        pltpu.make_async_copy(f.at[0, s, 0], E.at[s, :, 0:NP, E_ROWS], in_sem.at[s]).start()
        pltpu.make_async_copy(f.at[0, s, 1], H.at[s, :, 1 : NP + 1, H_ROWS], in_sem.at[s]).start()
        if s == 0:
            load_eps = pltpu.make_async_copy(ie, k, in_sem.at[2])
            load_eps.start()
    load_spectra = pltpu.make_async_copy(sp, so, in_sem.at[4])
    load_spectra.start()

    for s in range(2):
        for c in range(3):
            for z in range(NP):
                E[s, c, z, N:PAD] = jnp.zeros((PAD - N, N), F32)
                H[s, c, z + 1, 0:8] = jnp.zeros((8, N), F32)
        for c in range(2):
            e0h[s, c, 0:8] = jnp.zeros((8, N), F32)
            keep[s, c, 0:8] = jnp.zeros((8, N), F32)
    dz[N:PAD] = jnp.zeros((PAD - N, N), F32)

    @pl.when(slab == 0)
    def _():
        p1r[...] = jnp.zeros_like(p1r)
        p2r[...] = jnp.zeros_like(p2r)
        epsl[...] = jnp.zeros_like(epsl)

    @pl.when(slab == ns - 1)
    def _():
        e0h[...] = jnp.zeros_like(e0h)
        qr[...] = jnp.zeros_like(qr)
        epsu[...] = jnp.zeros_like(epsu)

    def down(src, dst, i):
        return send(src, dst, dn_s, dn_r.at[i], slab - 1, ang)

    def up(src, dst, i):
        return send(src, dst, up_s, up_r.at[i], slab + 1, ang)

    def send_outer(s, src, dst, neighbour, far, relay, exists, send_sem, recv_sem):
        pl.when(jnp.logical_and(exists, slab != far))(
            lambda: send(src.at[s], dst.at[s], send_sem, recv_sem.at[s], neighbour, ang).start())

        @pl.when(slab == far)
        def _():
            for c in range(2):
                if (s, c) in RELAYED:
                    send(src.at[s, c], rb.at[RELAYED.index((s, c))], send_sem, rl_r.at[RELAYED.index((s, c))], relay, ang).start()
            for c in range(2):
                if (s, c) not in RELAYED:
                    send(src.at[s, c], dst.at[s, c], send_sem, recv_sem.at[s], neighbour, ang).start()

    def send_q(s):
        send_outer(s, qs, qr, slab - 1, hi_design, relay_down, has_below, dn_s, dn_r)

    def send_p2(s):
        send_outer(s, p2s, p2r, slab + 1, lo_design, relay_up, has_above, up_s, up_r)

    def pass_on():
        for relay, dst, sems, d in ((relay_up, p2r, up_r, hi_design), (relay_down, qr, dn_r, lo_design)):
            @pl.when(slab == relay)
            def _():
                for i, (s, c) in enumerate(RELAYED):
                    wait_bytes(rb.at[i], rl_r.at[i])
                    send(rb.at[i], dst.at[s, c], rl_s, sems.at[s], d, ang).start()

    def h_new(s, z, top):
        ex, ey, ez = (E[s, c, z, E_ROWS] for c in range(3))
        if top:
            dzx, dzy = -ex, -ey
        else:
            dzx, dzy = E[s, 0, z + 1, E_ROWS] - ex, E[s, 1, z + 1, E_ROWS] - ey
        hx, hy, hz = (H[s, c, z + 1, H_ROWS] for c in range(3))
        hx = hx - 0.5 * ((next_y(ez) - ez) - dzy)
        hy = hy - 0.5 * (dzx - (E[s, 2, z, E_AHEAD] - ez))
        hz = hz - 0.5 * ((E[s, 1, z, E_AHEAD] - ey) - (next_y(ex) - ex))
        return hx, hy, hz

    def e_new(s, z, bottom):
        hx, hy, hz = (H[s, c, z + 1, H_ROWS] for c in range(3))
        if bottom:
            dzx, dzy = hx, hy
        else:
            dzx, dzy = hx - H[s, 0, z, H_ROWS], hy - H[s, 1, z, H_ROWS]
        kk = 0.5 * k[z]
        old = tuple(E[s, c, z, E_ROWS] for c in range(3))
        ex = old[0] + kk * ((hz - prev_y(hz)) - dzy)
        ey = old[1] + kk * (dzx - (hz - H[s, 2, z + 1, H_BEHIND]))
        ez = old[2] + kk * ((hy - H[s, 1, z + 1, H_BEHIND]) - (hx - prev_y(hx)))
        return old, (ex, ey, ez)

    def first_step(s):
        for z in range(NP):
            new = h_new(s, z, z == NP - 1)
            for c in range(3):
                H[s, c, z + 1, H_ROWS] = new[c]
        for c in range(2):
            p1s[s, c] = new[c]
        for z in range(NP):
            _, new = e_new(s, z, z == 0)
            for c in range(3):
                E[s, c, z, E_ROWS] = new[c]
                if z == 0 and c < 2:
                    qs[s, c] = new[c]
        new = h_new(s, NP - 1, True)
        for c in range(2):
            p2s[s, c] = new[c]

    edge = jnp.where(has_below, 0.5, 0.0).astype(F32)

    def fix_above(s):
        dx, dy = 0.5 * e0h[s, 1, H_ROWS], -0.5 * e0h[s, 0, H_ROWS]
        hx, hy = H[s, 0, NP, H_ROWS] + dx, H[s, 1, NP, H_ROWS] + dy
        H[s, 0, NP, H_ROWS] = hx
        H[s, 1, NP, H_ROWS] = hy
        k3 = 0.5 * k[NP - 1]
        E[s, 0, NP - 1, E_ROWS] = E[s, 0, NP - 1, E_ROWS] - k3 * dy
        E[s, 1, NP - 1, E_ROWS] = E[s, 1, NP - 1, E_ROWS] + k3 * dx
        E[s, 2, NP - 1, E_ROWS] = E[s, 2, NP - 1, E_ROWS] + k3 * (
            (dy + 0.5 * e0h[s, 0, H_BEHIND]) - (dx - prev_y(dx)))
        ku = 0.5 * epsu[...]
        E[s, 0, NP, E_ROWS] = qr[s, 0] + ku * hy
        E[s, 1, NP, E_ROWS] = qr[s, 1] - ku * hx

    def fix_below(s):
        dx, dy = edge * keep[s, 1, H_ROWS], -edge * keep[s, 0, H_ROWS]
        k0, kl = 0.5 * k[0], 0.5 * epsl[...]
        d = kl * ((dy + edge * keep[s, 0, H_BEHIND]) - (dx - prev_y(dx)))
        dz[E_ROWS] = d
        ex = E[s, 0, 0, E_ROWS] + k0 * (p1r[s, 1] + dy)
        ey = E[s, 1, 0, E_ROWS] - k0 * (p1r[s, 0] + dx)
        E[s, 0, 0, E_ROWS] = ex
        E[s, 1, 0, E_ROWS] = ey
        H[s, 0, 0, H_ROWS] = p2r[s, 0] + dx - 0.5 * (next_y(d) - d) + (edge * ey - 0.5 * kl * dx)
        H[s, 1, 0, H_ROWS] = p2r[s, 1] + dy + 0.5 * (dz[E_AHEAD] - d) - (edge * ex + 0.5 * kl * dy)

    def second_h(s, planes):
        for z in planes:
            new = h_new(s, z, False)
            for c in range(3):
                H[s, c, z + 1, H_ROWS] = new[c]
                fo[0, s, 1, c, z] = new[c]

    def second_e(s, planes):
        c0, s0, c1, s1 = (op(jnp.full((1, N), ph[t], F32)) for t in range(2) for op in (jnp.cos, jnp.sin))
        for z in planes:
            old, new = e_new(s, z, False)
            total = jnp.zeros((N, N), F32)
            for c in range(3):
                fo[0, s, 0, c, z] = new[c]
                re = so[0, s, 0, c, z] + old[c] * c0 + new[c] * c1
                im = so[0, s, 1, c, z] + old[c] * s0 + new[c] * s1
                so[0, s, 0, c, z] = re
                so[0, s, 1, c, z] = im
                if s == 1:
                    total = total + so[0, 0, 0, c, z] * re - so[0, 0, 1, c, z] * im
            if s == 1:
                dens[z] = total

    def lower_planes(s):
        @pl.when(has_below)
        def _():
            if s == 0:
                wait_bytes(epsl, up_r.at[2])
            wait_bytes(fo.at[0, s, 0, 0], up_r.at[s])

        fix_below(s)
        second_h(s, (0,))
        second_e(s, (0, 1))

    def upper_planes(s):
        @pl.when(has_above)
        def _():
            if s == 0:
                wait_bytes(epsu, dn_r.at[2])
            wait_bytes(fo.at[0, s, 0, 0], dn_r.at[s])

        fix_above(s)
        second_h(s, (2, 3))
        second_e(s, (2, 3))

    wait_bytes(so.at[0, 0], in_sem.at[0])
    load_eps.wait()
    load_keep.wait()
    first_step(0)
    incoming = jnp.where(has_below, 1, 0) + jnp.where(has_above, 1, 0)
    incoming = incoming + jnp.where(is_design, 1, 2 + na - 1)
    incoming = incoming + jnp.where(jnp.logical_or(slab == lo_design - 1, slab == hi_design + 1), na - 1, 0)
    pl.semaphore_wait(bar, incoming)

    @pl.when(jnp.logical_not(is_design))
    def _():
        for d in (lo_design, hi_design):
            pl.semaphore_signal(ready, inc=1, device_id=(d, ang), device_id_type=MESH)

    @pl.when(has_below)
    def _():
        down(k.at[0], epsu, 2).start()
        for s in range(2):
            down(keep.at[s, :, H_ROWS], e0h.at[s, :, H_ROWS], s).start()

    @pl.when(has_above)
    def _():
        up(k.at[NP - 1], epsl, 2).start()
        up(p1s.at[0], p1r.at[0], 0).start()

    send_q(0)
    send_p2(0)
    wait_bytes(so.at[0, 1], in_sem.at[1])
    first_step(1)
    pl.when(has_above)(lambda: up(p1s.at[1], p1r.at[1], 1).start())
    send_q(1)
    send_p2(1)
    pass_on()
    for s in range(2):
        second_h(s, (1,))
    fy[...] = jnp.concatenate([filter_matrix(False).astype(jnp.bfloat16)] * 3, axis=0)
    mx[...] = jnp.concatenate([(filter_matrix(True) * (0.5 / na)).astype(jnp.bfloat16)] * 3, axis=1)
    load_spectra.wait()

    def to_owner(part, side, owner):
        return send(gbuf.at[part, :, pl.ds(owner * cols, cols)], r1.at[part, pl.ds(side * HALF, HALF)],
                    g1_s, g1_r.at[part], owner, ang)

    def spread_density(part, first, side):
        planes = dens[first : first + HALF].reshape(HALF * N, N)
        along_y = jnp.dot(jnp.concatenate(three_parts(planes), axis=1), fy[...], preferred_element_type=F32)
        beside = jnp.concatenate([along_y[z * N : (z + 1) * N] for z in range(HALF)], axis=1)
        both = jnp.dot(mx[...], jnp.concatenate(three_parts(beside), axis=0), preferred_element_type=F32)
        for z in range(HALF):
            gbuf[part, z] = both[:, z * N : (z + 1) * N]
        d = (lo_design, hi_design)[side]
        for owner in (*range(1, ns, 2), *range(0, ns, 2)):
            if owner != d:
                to_owner(part, side, owner).start()
        r1[part, side * HALF : (side + 1) * HALF] = gbuf[part, :, d * cols : (d + 1) * cols]

    def beside_core(planes_below):
        for odd, planes in ((1, lower_planes), (0, upper_planes)):
            @pl.when(slab % 2 == (odd if planes_below else 1 - odd))
            def _():
                for s in range(2):
                    planes(s)

    beside_core(True)
    pl.when(is_design)(lambda: pl.semaphore_wait(ready, ns - 2))
    for side, d in enumerate((lo_design, hi_design)):
        pl.when(slab == d)(functools.partial(spread_density, 0, HALF * side, side))

    @pl.when(slab == lo_design)
    def _():
        for s in range(2):
            upper_planes(s)
        spread_density(1, HALF, 0)

    @pl.when(slab == hi_design)
    def _():
        for s in range(2):
            lower_planes(s)
        spread_density(1, 0, 1)

    for part in (0, 1):
        pl.when(is_design)(lambda: wait_bytes(r1.at[part, pl.ds(0, HALF)], g1_r.at[part]))
        pl.when(jnp.logical_not(is_design))(lambda: wait_bytes(r1.at[part], g1_r.at[part]))
        for j in range(1, na):
            send(r1.at[part], r2.at[part, ang], g2_s, g2_r.at[part], slab, lax.rem(ang + j, na)).start()
        r2[part, ang] = r1[part]

    pl.when(jnp.logical_not(is_design))(lambda: beside_core(False))

    for part in (0, 1):
        wait_bytes(r2.at[part, pl.ds(0, na - 1)], g2_r.at[part])
        total = r2[part, 0]
        for j in range(1, na):
            total = total + r2[part, j]
        if part == 0:
            g[0:HALF] = total[0:HALF]
            g[NP + HALF :] = total[HALF:]
        else:
            g[HALF : NP + HALF] = total

    wait_bytes(r2.at[:, pl.ds(0, na - 1)], g2_s)
    nine_planes = E.at[0, 0:3, 0:3, E_ROWS]
    pl.when(has_below)(lambda: wait_bytes(nine_planes, dn_s))
    pl.when(has_above)(lambda: wait_bytes(nine_planes, up_s))
    pl.when(jnp.logical_or(slab == relay_up, slab == relay_down))(lambda: wait_bytes(rb, rl_s))
    pl.when(is_design)(lambda: wait_bytes(gbuf.at[:, :, pl.ds(0, N - cols)], g1_s))


def write_out(a, b, c, x, y, z, sem):
    copies = [pltpu.make_async_copy(p, q, sem.at[i]) for i, (p, q) in enumerate(((a, x), (b, y), (c, z)))]
    for copy in copies:
        copy.start()
    for copy in copies:
        copy.wait()


def per_device(fields, spectra, inv_eps, step_phase):
    ns, na = lax.axis_size("slab"), lax.axis_size("angle")
    cols = N // ns
    shape = fields.shape
    vmem = pl.BlockSpec(memory_space=pltpu.VMEM)
    hbm = pl.BlockSpec(memory_space=pltpu.HBM)
    outs = (shape, shape, (2 * NP, cols, N))
    dma = pltpu.SemaphoreType.DMA
    planes = pltpu.VMEM((2, 2, N, N), F32)
    results = pl.pallas_call(
        functools.partial(kernel, ns, na),
        out_shape=[pltpu.VMEM(s, F32) for s in outs],
        in_specs=[hbm, hbm, hbm, pl.BlockSpec(memory_space=pltpu.SMEM)],
        out_specs=[vmem] * 3,
        scratch_shapes=[
            pltpu.VMEM((2, 3, NP + 1, PAD, N), F32),
            pltpu.VMEM((2, 3, NP + 1, PAD, N), F32),
            pltpu.VMEM((NP, N, N), F32),
            pltpu.VMEM((2, 2, PAD, N), F32),
            pltpu.VMEM((2, 2, PAD, N), F32),
            pltpu.VMEM((PAD, N), F32),
            planes, planes, planes, planes, planes, planes,
            pltpu.VMEM((N, N), F32),
            pltpu.VMEM((N, N), F32),
            pltpu.VMEM((NP, N, N), F32),
            pltpu.VMEM((3 * N, N), jnp.bfloat16),
            pltpu.VMEM((N, 3 * N), jnp.bfloat16),
            pltpu.VMEM((2, HALF, N, N), F32),
            pltpu.VMEM((2, NP, cols, N), F32),
            pltpu.VMEM((2, na, NP, cols, N), F32),
            pltpu.VMEM((len(RELAYED), N, N), F32),
            dma((5,)), dma, dma((3,)), dma, dma((3,)), dma, dma((len(RELAYED),)), dma, dma((2,)), dma, dma((2,)),
            pltpu.SemaphoreType.REGULAR,
        ],
        compiler_params=pltpu.CompilerParams(
            collective_id=0, has_side_effects=True, vmem_limit_bytes=48 * 2**20),
        name="steps",
    )(fields, spectra, inv_eps, step_phase)
    return tuple(pl.pallas_call(
        write_out,
        out_shape=[jax.ShapeDtypeStruct(s, F32) for s in outs],
        in_specs=[vmem] * 3,
        out_specs=[pl.BlockSpec(memory_space=pl.ANY)] * 3,
        scratch_shapes=[dma((3,))],
        compiler_params=pltpu.CompilerParams(has_side_effects=True, vmem_limit_bytes=2**20),
        name="write_out",
    )(*(pltpu.with_memory_space_constraint(r, pltpu.VMEM) for r in results)))


def solution(mesh):
    cells = P("angle", None, None, None, "slab", None, None)
    return jax.shard_map(
        per_device,
        mesh=mesh,
        in_specs=(cells, cells, P("slab", None, None), P()),
        out_specs=(cells, cells, P(None, "slab", None)),
        check_vma=False,
    )
```
